32 devices in a mesh: ctx: 8 (over y, x, core), tp: 4 (over z).
Axes of the slice: x: 2, y: 2, z: 4, core: 2. Of those that a mesh axis runs over, the one named last changes fastest.
Arguments:
- query: bfloat16 [2048, 5120], P('ctx', 'tp'), may hold values from -6 to 6
- key_projected: bfloat16 [2048, 1024], P('ctx', 'tp'), may hold values from -6 to 6
- value: bfloat16 [2048, 1024], P('ctx', 'tp'), may hold values from -6 to 6
- attention_output: bfloat16 [2048, 5120], P('ctx', 'tp'), may hold values from -6 to 6
- output_gradient: bfloat16 [2048, 5120], P('ctx', 'tp'), may hold values from -6 to 6
- lse: float32 [40, 2048], P('tp', 'ctx'), may hold values from 4 to 7
- block_mask: int32 [16, 16], replicated, may hold values from 0 to 1, as said below
- positions: int32 [2048], P('ctx'), may hold values from 0 to 1023, as said below
- segments: int32 [2048], replicated, may hold values from 0 to 31, as said below
- w_query: bfloat16 [5120, 5120], P(None, 'tp'), may hold values from -0.078125 to 0.078125
- key_weight: bfloat16 [5120, 1024], P(None, 'tp'), may hold values from -0.078125 to 0.078125
- value_weight: bfloat16 [5120, 1024], P(None, 'tp'), may hold values from -0.078125 to 0.078125
Outputs:
- input_grad_t: bfloat16 [5120, 2048], P('tp', 'ctx')
The draws below stay inside these ranges and needn't reach their ends.
Inputs may be any that keep to these rules, and one draw needn't show every extreme that they name: block_mask[a, b] is 1 exactly when tile b is tile a or an ancestor of tile a in a forest of tiles in which every tile's parent is an earlier tile. `positions`: a token's position is 128 times its tile's number of ancestors plus its offset from the first token of its segment within the tile. `segments`: never falling along the tokens; one segment a tile, except that a tile that is no other tile's ancestor may hold two, the second beginning inside it.
All inputs are finite; a program needn't handle non-finite values.
Results may differ from the reference program's by a relative error of at most 0.0065.
The reference program's roundings to bfloat16 on the way count: a program that leaves them out, or rounds other values in their place, can miss the bound.
Values may be sent and summed in bfloat16 or wider, within the bound.
A program may use at most 128 MiB of HBM per device.

```python
import jax
import jax.numpy as jnp
from jax import lax

MODEL_WIDTH = 5120
QUERY_HEADS = 40
KEY_VALUE_HEADS = 8
HEAD_SIZE = 128
TILE = 128
PACKED_TOKENS = 2048


def tree_parts(key):
    tiles = PACKED_TOKENS // TILE
    levels = 8
    first, second, third = jax.random.split(key, 3)
    index = jnp.arange(tiles).astype(jnp.int32)
    raw = jax.random.randint(first, (tiles,), 0, 1 << 30)
    choices_count = jnp.maximum(index - 1, 0) // levels + 1
    parent = index - 1 - levels * (raw % choices_count)
    parent = jnp.where(index % levels == 0, index, parent).astype(jnp.int32)
    ancestors = ((index[None, :] == parent[:, None]) | (index[None, :] == index[:, None])).astype(jnp.int32)
    for _ in range(int(tiles).bit_length() + 1):
        ancestors = (jnp.dot(ancestors, ancestors) > 0).astype(jnp.int32)
    has_child = jnp.zeros((tiles,), jnp.int32).at[parent].max(jnp.where(parent != index, 1, 0).astype(jnp.int32))
    cut_point = jax.random.randint(second, (tiles,), 1, TILE)
    split_tile = (jax.random.randint(third, (tiles,), 0, 2) == 1) & (has_child == 0) & (index != levels - 1)
    split_tile = split_tile | (index == tiles - 1)
    depth = jnp.sum(ancestors, axis=1) - 1
    offset = jnp.arange(TILE).astype(jnp.int32)
    later = split_tile[:, None] & (offset[None, :] >= cut_point[:, None])
    seg_ids = (2 * index[:, None] + later.astype(jnp.int32)).reshape(-1)
    pos_ids = (TILE * depth[:, None] + jnp.where(later, offset[None, :] - cut_point[:, None], offset[None, :])).reshape(-1)
    return (ancestors.astype(jnp.int32), pos_ids.astype(jnp.int32), seg_ids.astype(jnp.int32))


def draw_block_mask(key, part):
    ancestors, pos_ids, seg_ids = tree_parts(key)
    return ancestors


def draw_positions(key, part):
    ancestors, pos_ids, seg_ids = tree_parts(key)
    return pos_ids


def draw_segments(key, part):
    ancestors, pos_ids, seg_ids = tree_parts(key)
    return seg_ids


def block_scale(rng, shape, shards, low, largest):
    def one(axis_at, shards_of):
        heights = jax.random.uniform(jax.random.fold_in(jax.random.fold_in(rng, 6), axis_at), (shards_of,), jnp.float32, low / len(shards), largest / len(shards))
        return jnp.repeat(jnp.exp(heights), shape[axis_at] // shards_of).reshape((-1,) + (1,) * (len(shape) - axis_at - 1))

    factor_of = one(*shards[0])
    for cut in shards[1:]:
        factor_of = factor_of * one(*cut)
    return factor_of


def gaussian(stream_key, shape, deviation, bound, pieces=(), held_as=jnp.bfloat16):
    values = jax.random.normal(stream_key, shape, jnp.float32) * deviation
    if len(pieces) > 0:
        values = block_scale(stream_key, shape, pieces, -0.22, 0.18) * values
    return jnp.clip(values, min=-bound, max=bound).astype(held_as)


def setup_inputs(seed: int = 0) -> dict:
    arg_keys = jax.random.split(jax.random.key(seed), 13)
    return {
        "query": gaussian(arg_keys[0], (PACKED_TOKENS, QUERY_HEADS * HEAD_SIZE), 1.0, 6.0, ((0, 8), (1, 4))),
        "key_projected": gaussian(arg_keys[1], (PACKED_TOKENS, KEY_VALUE_HEADS * HEAD_SIZE), 1.0, 6.0, ((0, 8), (1, 4))),
        "value": gaussian(arg_keys[2], (PACKED_TOKENS, KEY_VALUE_HEADS * HEAD_SIZE), 1.0, 6.0, ((0, 8), (1, 4))),
        "attention_output": gaussian(arg_keys[3], (PACKED_TOKENS, QUERY_HEADS * HEAD_SIZE), 1.0, 6.0, ((0, 8), (1, 4))),
        "output_gradient": gaussian(arg_keys[4], (PACKED_TOKENS, QUERY_HEADS * HEAD_SIZE), 1.0, 6.0, ((0, 8), (1, 4))),
        "lse": jnp.clip(4.0 + 3.0 * jax.random.uniform(arg_keys[5], (QUERY_HEADS, PACKED_TOKENS), jnp.float32) ** block_scale(arg_keys[5], (QUERY_HEADS, PACKED_TOKENS), ((0, 4), (1, 8)), -0.2, 0.2), 4.0, 7.0),
        "block_mask": draw_block_mask(jax.random.fold_in(arg_keys[12], 71), 0),
        "positions": draw_positions(jax.random.fold_in(arg_keys[12], 71), 0),
        "segments": draw_segments(jax.random.fold_in(arg_keys[12], 71), 0),
        "w_query": gaussian(arg_keys[9], (MODEL_WIDTH, QUERY_HEADS * HEAD_SIZE), MODEL_WIDTH ** -0.5, 0.078125, ((1, 4),)),
        "key_weight": gaussian(arg_keys[10], (MODEL_WIDTH, KEY_VALUE_HEADS * HEAD_SIZE), MODEL_WIDTH ** -0.5, 0.078125, ((1, 4),)),
        "value_weight": gaussian(arg_keys[11], (MODEL_WIDTH, KEY_VALUE_HEADS * HEAD_SIZE), MODEL_WIDTH ** -0.5, 0.078125, ((1, 4),)),
    }


rope_base = 1000000.0


def rope_tables(positions, head_dim):
    half = head_dim // 2
    exponent = jnp.arange(half).astype(jnp.float32) * (2.0 / head_dim)
    inverse = jnp.power(jnp.float32(rope_base), -exponent)
    angles = positions.astype(jnp.float32)[:, None] * inverse[None, :]
    cosine_table = jnp.cos(angles)
    sine_table = jnp.sin(angles)
    return jnp.concatenate([cosine_table, cosine_table], 1), jnp.concatenate([sine_table, sine_table], 1)


def rotate_forward(values, cosine_table, sine_table):
    half = values.shape[-1] // 2
    turned = jnp.concatenate([-values[..., half:], values[..., :half]], -1)
    return values * cosine_table[:, None, :] + turned * sine_table[:, None, :]


def unrotate_halves(grads, cosine_table, sine_table):
    half = grads.shape[-1] // 2
    scaled = grads * sine_table[:, None, :]
    turned = jnp.concatenate([scaled[..., half:], -scaled[..., :half]], -1)
    return grads * cosine_table[:, None, :] + turned


def pair_mask(block_mask, segments, q_start, q_count, k_start, k_count, tile):
    q_start = jnp.asarray(q_start).astype(jnp.int32)
    k_start = jnp.asarray(k_start).astype(jnp.int32)
    table = lax.dynamic_slice(block_mask, (q_start // tile, k_start // tile), (q_count // tile, k_count // tile))
    wide = jnp.broadcast_to(table[:, None, :, None], (q_count // tile, tile, k_count // tile, tile)).reshape(q_count, k_count) > 0
    q_index = q_start + jnp.arange(q_count).astype(jnp.int32)
    k_index = k_start + jnp.arange(k_count).astype(jnp.int32)
    seg_query = lax.dynamic_slice_in_dim(segments, q_start, q_count)
    seg_key = lax.dynamic_slice_in_dim(segments, k_start, k_count)
    same_tile = (q_index[:, None] // tile) == (k_index[None, :] // tile)
    inner = (k_index[None, :] <= q_index[:, None]) & (seg_query[:, None] == seg_key[None, :])
    return wide & (jnp.logical_not(same_tile) | inner)


def reference(query, key_projected, value, attention_output, output_gradient, lse, block_mask, positions, segments, w_query, key_weight, value_weight):
    grand_total = PACKED_TOKENS
    query_groups = QUERY_HEADS // KEY_VALUE_HEADS
    logit_scale = HEAD_SIZE ** -0.5
    cosine_table, sine_table = rope_tables(positions, HEAD_SIZE)
    query_rotated = rotate_forward(query.astype(jnp.float32).reshape(grand_total, QUERY_HEADS, HEAD_SIZE), cosine_table, sine_table).astype(jnp.bfloat16)
    query_rotated = query_rotated.reshape(grand_total, KEY_VALUE_HEADS, query_groups, HEAD_SIZE)
    key_rotated = rotate_forward(key_projected.astype(jnp.float32).reshape(grand_total, KEY_VALUE_HEADS, HEAD_SIZE), cosine_table, sine_table).astype(jnp.bfloat16)
    head_gradient = output_gradient.reshape(grand_total, KEY_VALUE_HEADS, query_groups, HEAD_SIZE)
    row_dot_delta = jnp.sum(head_gradient.astype(jnp.float32) * attention_output.reshape(grand_total, KEY_VALUE_HEADS, query_groups, HEAD_SIZE).astype(jnp.float32), -1)
    row_logsumexp = lse.T.reshape(grand_total, KEY_VALUE_HEADS, query_groups)
    key_float = key_rotated.astype(jnp.float32)
    value_single = value.reshape(grand_total, KEY_VALUE_HEADS, HEAD_SIZE).astype(jnp.float32)

    def step(carry, index):
        start = (index * TILE).astype(jnp.int32)
        query_blk = lax.dynamic_slice_in_dim(query_rotated, start, TILE, 0).astype(jnp.float32)
        grad_blk = lax.dynamic_slice_in_dim(head_gradient, start, TILE, 0).astype(jnp.float32)
        lse_blk = lax.dynamic_slice_in_dim(row_logsumexp, start, TILE, 0)
        delta_blk = lax.dynamic_slice_in_dim(row_dot_delta, start, TILE, 0)
        allowed = pair_mask(block_mask, segments, start, TILE, 0, grand_total, TILE)
        scores = jnp.einsum('tkgd,skd->tkgs', query_blk, key_float) * logit_scale
        probs = jnp.where(allowed[:, None, None, :], jnp.exp(scores - lse_blk[..., None]), 0.0)
        dprobs = jnp.einsum('tkgd,skd->tkgs', grad_blk, value_single)
        dscore = probs * (dprobs - delta_blk[..., None])
        probs_bf = lax.optimization_barrier(probs.astype(jnp.bfloat16)).astype(jnp.float32)
        dscore_bf = lax.optimization_barrier(dscore.astype(jnp.bfloat16)).astype(jnp.float32)
        query_part = jnp.einsum('tkgs,skd->tkgd', dscore_bf, key_float) * logit_scale
        key_accumulator = carry[0] + jnp.einsum('tkgs,tkgd->skd', dscore_bf, query_blk)
        value_accumulator = carry[1] + jnp.einsum('tkgs,tkgd->skd', probs_bf, grad_blk)
        return (key_accumulator, value_accumulator), query_part

    zero_filled = jnp.zeros((grand_total, KEY_VALUE_HEADS, HEAD_SIZE), jnp.float32)
    (key_accumulator, value_accumulator), query_parts = lax.scan(step, (zero_filled, zero_filled), jnp.arange(grand_total // TILE).astype(jnp.int32))
    query_rot_grad = query_parts.reshape(grand_total, QUERY_HEADS, HEAD_SIZE)
    query_grad = unrotate_halves(query_rot_grad, cosine_table, sine_table).astype(jnp.bfloat16).reshape(grand_total, QUERY_HEADS * HEAD_SIZE)
    key_gradient = unrotate_halves(key_accumulator * logit_scale, cosine_table, sine_table).astype(jnp.bfloat16).reshape(grand_total, KEY_VALUE_HEADS * HEAD_SIZE)
    value_gradient = value_accumulator.astype(jnp.bfloat16).reshape(grand_total, KEY_VALUE_HEADS * HEAD_SIZE)
    result = jnp.dot(w_query, query_grad.T, preferred_element_type=jnp.float32)
    result = result + jnp.dot(key_weight, key_gradient.T, preferred_element_type=jnp.float32)
    result = result + jnp.dot(value_weight, value_gradient.T, preferred_element_type=jnp.float32)
    return result.astype(jnp.bfloat16)
```

```python
import functools

import jax
import jax.numpy as jnp
from jax import lax
from jax.experimental import pallas as pl
from jax.experimental.pallas import tpu as pltpu
from jax.sharding import PartitionSpec as P

QUERY_HEADS = 40
KEY_VALUE_HEADS = 8
HEAD_SIZE = 128
TILE = 128
GROUP = QUERY_HEADS // KEY_VALUE_HEADS
SCALE = HEAD_SIZE ** (-0.5)
MESH = pl.DeviceIdType.MESH
VMEM_BYTES = 56 * 1024 * 1024

rope_base = 1000000.0


def rope_tables(positions, head_dim):
    half = head_dim // 2
    exponent = jnp.arange(half).astype(jnp.float32) * (2.0 / head_dim)
    inverse = jnp.power(jnp.float32(rope_base), -exponent)
    angles = positions.astype(jnp.float32)[:, None] * inverse[None, :]
    cosine_table = jnp.cos(angles)
    sine_table = jnp.sin(angles)
    return (
        jnp.concatenate([cosine_table, cosine_table], 1),
        jnp.concatenate([-sine_table, sine_table], 1),
    )


def swap_halves(x):
    half = HEAD_SIZE // 2
    return jnp.concatenate([x[..., half:], x[..., :half]], -1)


def dot(a, b, dims=((1,), (0,))):
    return lax.dot_general(a, b, (dims, ((), ())), preferred_element_type=jnp.float32)


def attention_kernel(
    start_ref, mask_ref, q_ref, do_ref, lse_ref, delta_ref, cos_ref, sin_ref, kv_ref, segq_ref, segk_ref,
    dq_ref, dkv_ref, qs, dos, qt_s, dot_s, lse_s, delta_s, dqt,
):
    tokens = q_ref.shape[0]
    kv_local = kv_ref.shape[1] // (2 * HEAD_SIZE)
    q_tiles = tokens // TILE
    wide = GROUP * TILE
    first_tile = start_ref[0]
    dkv_ref[...] = jnp.zeros_like(dkv_ref)
    dqt[...] = jnp.zeros_like(dqt)
    for t in range(q_tiles):
        rows = slice(t * TILE, (t + 1) * TILE)
        cosine = cos_ref[rows, :]
        sine = sin_ref[rows, :]
        for h in range(kv_local * GROUP):
            c, g = h // GROUP, h % GROUP
            part = slice(g * TILE, (g + 1) * TILE)
            cols = slice(h * HEAD_SIZE, (h + 1) * HEAD_SIZE)
            x = q_ref[rows, cols].astype(jnp.float32)
            x = x * cosine + pltpu.roll(x, HEAD_SIZE // 2, 1) * sine
            xb = x.astype(jnp.bfloat16)
            qs[t, c, part, :] = xb
            qt_s[t, c, :, part] = xb.astype(jnp.float32).T.astype(jnp.bfloat16)
            y = do_ref[rows, cols]
            dos[t, c, part, :] = y
            dot_s[t, c, :, part] = y.astype(jnp.float32).T.astype(jnp.bfloat16)
            lse_s[t, c, :, part] = lse_ref[h : h + 1, rows]
            delta_s[t, c, :, part] = delta_ref[h : h + 1, rows]

    def pair(t, k_tile, allowed):
        k_rows = pl.ds(pl.multiple_of(k_tile * TILE, TILE), TILE)
        for c in range(kv_local):
            key_cols = slice(c * HEAD_SIZE, (c + 1) * HEAD_SIZE)
            val_cols = slice((kv_local + c) * HEAD_SIZE, (kv_local + c + 1) * HEAD_SIZE)
            k = kv_ref[k_rows, key_cols]
            v = kv_ref[k_rows, val_cols]
            scores = dot(k, qt_s[t, c]) * SCALE
            probs = jnp.exp(scores - lse_s[t, c])
            if allowed is not None:
                probs = jnp.where(allowed, probs, 0.0)
            dscore = probs * (dot(v, dot_s[t, c]) - delta_s[t, c])
            pb = probs.astype(jnp.bfloat16)
            db = dscore.astype(jnp.bfloat16)
            dkv_ref[k_rows, key_cols] += dot(db, qs[t, c])
            dkv_ref[k_rows, val_cols] += dot(pb, dos[t, c])
            kt = k.astype(jnp.float32).T.astype(jnp.bfloat16)
            dqt[t, c] += dot(kt, db)

    for t in range(q_tiles):
        own = first_tile + t

        @pl.loop(0, own)
        def _(k_tile):
            @pl.when(mask_ref[own, k_tile] > 0)
            def _():
                pair(t, k_tile, None)

        row = lax.broadcasted_iota(jnp.int32, (TILE, TILE), 0)
        col = lax.broadcasted_iota(jnp.int32, (TILE, TILE), 1)
        seg_k = segk_ref[t * TILE : (t + 1) * TILE, :]
        seg_q = segq_ref[:, t * TILE : (t + 1) * TILE]
        inner = jnp.where((row <= col) & (seg_k == seg_q), 1.0, 0.0)
        inner = jnp.concatenate([inner] * GROUP, 1) > 0.5
        pair(t, own, inner)

        rows = slice(t * TILE, (t + 1) * TILE)
        cosine = cos_ref[rows, :]
        sine = sin_ref[rows, :]
        for h in range(kv_local * GROUP):
            c, g = h // GROUP, h % GROUP
            x = (dqt[t, c, :, g * TILE : (g + 1) * TILE] * SCALE).T
            x = x * cosine - pltpu.roll(x, HEAD_SIZE // 2, 1) * sine
            dq_ref[rows, h * HEAD_SIZE : (h + 1) * HEAD_SIZE] = x.astype(jnp.bfloat16)


def attention(first_tile, block_mask, query, grad, lse, delta, cosine, sine, kv_whole, seg_row):
    tokens = query.shape[0]
    kv_local = kv_whole.shape[1] // (2 * HEAD_SIZE)
    q_tiles = tokens // TILE
    wide = GROUP * TILE
    vm = pl.BlockSpec(memory_space=pltpu.VMEM)
    sm = pl.BlockSpec(memory_space=pltpu.SMEM)
    return pl.pallas_call(
        attention_kernel,
        out_shape=(
            jax.ShapeDtypeStruct(query.shape, jnp.bfloat16),
            jax.ShapeDtypeStruct(kv_whole.shape, jnp.float32),
        ),
        in_specs=[sm, sm] + [vm] * 9,
        out_specs=(vm, vm),
        scratch_shapes=[
            pltpu.VMEM((q_tiles, kv_local, wide, HEAD_SIZE), jnp.bfloat16),
            pltpu.VMEM((q_tiles, kv_local, wide, HEAD_SIZE), jnp.bfloat16),
            pltpu.VMEM((q_tiles, kv_local, HEAD_SIZE, wide), jnp.bfloat16),
            pltpu.VMEM((q_tiles, kv_local, HEAD_SIZE, wide), jnp.bfloat16),
            pltpu.VMEM((q_tiles, kv_local, 1, wide), jnp.float32),
            pltpu.VMEM((q_tiles, kv_local, 1, wide), jnp.float32),
            pltpu.VMEM((q_tiles, kv_local, HEAD_SIZE, wide), jnp.float32),
        ],
        compiler_params=pltpu.CompilerParams(vmem_limit_bytes=VMEM_BYTES),
        name="attention",
    )(first_tile, block_mask, query, grad, lse, delta, cosine, sine, kv_whole, seg_row, seg_row.reshape(tokens, 1))


def project_kernel(
    n, dq_ref, dkv_ref, wq_ref, wk_ref, wv_ref, out_ref,
    wq, wk, wv, acc, send, send_scale, recv, recv_scale,
    w_sem, send_sem, recv_sem, send_scale_sem, recv_scale_sem,
):
    me = lax.axis_index("tp")
    chunk_rows = out_ref.shape[0]
    sub_rows = acc.shape[0]
    subs = chunk_rows // sub_rows
    steps = 2 * (n - 1) * subs

    def plan(i):
        way = lax.rem(i, 2)
        rightward = jnp.where(me < n // 2, 1 - way, way)
        sub = lax.rem(i // 2, subs)
        step = i // (2 * subs)
        chunk = jnp.where(rightward == 1, n - 1 - step, step)
        active = jnp.where(rightward == 1, chunk > me, chunk < me)
        return rightward, chunk, sub, active

    def weight_copies(chunk, sub):
        at = chunk * subs + sub
        rows = pl.ds(pl.multiple_of(at * sub_rows, sub_rows), sub_rows)
        return [
            pltpu.make_async_copy(src.at[rows, :], dst.at[rows, :], w_sem.at[j, at])
            for j, (src, dst) in enumerate(((wq_ref, wq), (wk_ref, wk), (wv_ref, wv)))
        ]

    def remote(rightward, chunk, sub):
        slot = chunk * subs + sub
        to = jnp.where(rightward == 1, jnp.minimum(me + 1, n - 1), jnp.maximum(me - 1, 0))
        return [
            pltpu.make_async_remote_copy(
                src_ref=s.at[slot],
                dst_ref=r.at[rightward, slot],
                send_sem=ss.at[slot],
                recv_sem=rs.at[rightward, slot],
                device_id={"tp": to},
                device_id_type=MESH,
            )
            for s, r, ss, rs in (
                (send, recv, send_sem, recv_sem),
                (send_scale, recv_scale, send_scale_sem, recv_scale_sem),
            )
        ]

    def own_term(chunk, sub):
        for copy in weight_copies(chunk, sub):
            copy.wait()
        at = chunk * subs + sub
        rows = pl.ds(pl.multiple_of(at * sub_rows, sub_rows), sub_rows)
        half = wk.shape[1]
        contract = ((1,), (1,))
        total = dot(wq[rows, :], dq_ref[...], contract)
        total = total + dot(wk[rows, :], dkv_ref[:, :half], contract)
        acc[...] = total + dot(wv[rows, :], dkv_ref[:, half:], contract)

    def add_received(rightward, chunk, sub):
        for copy in remote(rightward, chunk, sub):
            copy.wait_recv()
        slot = chunk * subs + sub
        scale = recv_scale[rightward, slot, 0:1, :]
        acc[...] += recv[rightward, slot].astype(jnp.int32).astype(jnp.float32) * scale

    @pl.loop(0, steps)
    def _(i):
        _, chunk, sub, active = plan(i)

        @pl.when(active)
        def _():
            for copy in weight_copies(chunk, sub):
                copy.start()

    @pl.loop(0, subs)
    def _(sub):
        for copy in weight_copies(me, sub):
            copy.start()

    barrier = pltpu.get_barrier_semaphore()

    @pl.when(me > 0)
    def _():
        pl.semaphore_signal(barrier, inc=1, device_id={"tp": jnp.maximum(me - 1, 0)}, device_id_type=MESH)

    @pl.when(me < n - 1)
    def _():
        pl.semaphore_signal(barrier, inc=1, device_id={"tp": jnp.minimum(me + 1, n - 1)}, device_id_type=MESH)

    peers = jnp.where(me > 0, 1, 0) + jnp.where(me < n - 1, 1, 0)
    pl.semaphore_wait(barrier, peers)

    @pl.loop(0, steps)
    def _(i):
        rightward, chunk, sub, active = plan(i)

        @pl.when(active)
        def _():
            own_term(chunk, sub)

            @pl.when(jnp.where(rightward == 1, me > 0, me < n - 1))
            def _():
                add_received(rightward, chunk, sub)

            slot = chunk * subs + sub
            largest = jnp.maximum(jnp.max(jnp.abs(acc[...]), axis=0, keepdims=True), 1e-30)
            send_scale[slot] = jnp.broadcast_to(largest * (1.0 / 32767.0), send_scale.shape[1:])
            coded = jnp.round(acc[...] * (32767.0 / largest))
            send[slot] = coded.astype(jnp.int32).astype(jnp.int16)
            for copy in remote(rightward, chunk, sub):
                copy.start()

    @pl.loop(0, subs)
    def _(sub):
        own_term(me, sub)

        @pl.when(me > 0)
        def _():
            add_received(1, me, sub)

        @pl.when(me < n - 1)
        def _():
            add_received(0, me, sub)

        rows = pl.ds(pl.multiple_of(sub * sub_rows, sub_rows), sub_rows)
        out_ref[rows, :] = acc[...].astype(jnp.bfloat16)

    @pl.loop(0, steps)
    def _(i):
        rightward, chunk, sub, active = plan(i)

        @pl.when(active)
        def _():
            for copy in remote(rightward, chunk, sub):
                copy.wait_send()


def project(n, dq, dkv, w_query, key_weight, value_weight):
    tokens = dq.shape[0]
    width = w_query.shape[0]
    chunk_rows = width // n
    sub_rows = 320 if chunk_rows % 320 == 0 else chunk_rows
    slots = width // sub_rows
    vm = pl.BlockSpec(memory_space=pltpu.VMEM)
    hbm = pl.BlockSpec(memory_space=pl.ANY)
    dma = pltpu.SemaphoreType.DMA
    return pl.pallas_call(
        functools.partial(project_kernel, n),
        out_shape=jax.ShapeDtypeStruct((chunk_rows, tokens), jnp.bfloat16),
        in_specs=[vm, vm, hbm, hbm, hbm],
        out_specs=vm,
        scratch_shapes=[
            pltpu.VMEM(w_query.shape, jnp.bfloat16),
            pltpu.VMEM(key_weight.shape, jnp.bfloat16),
            pltpu.VMEM(value_weight.shape, jnp.bfloat16),
            pltpu.VMEM((sub_rows, tokens), jnp.float32),
            pltpu.VMEM((slots, sub_rows, tokens), jnp.int16),
            pltpu.VMEM((slots, 8, tokens), jnp.float32),
            pltpu.VMEM((2, slots, sub_rows, tokens), jnp.int16),
            pltpu.VMEM((2, slots, 8, tokens), jnp.float32),
            dma((3, slots)),
            dma((slots,)),
            dma((2, slots)),
            dma((slots,)),
            dma((2, slots)),
        ],
        compiler_params=pltpu.CompilerParams(
            collective_id=2, has_side_effects=True, vmem_limit_bytes=VMEM_BYTES
        ),
        name="project",
    )(dq, dkv, w_query, key_weight, value_weight)


def local(
    n_ctx,
    n_tp,
    query,
    key_projected,
    value,
    attention_output,
    output_gradient,
    lse,
    block_mask,
    positions,
    segments,
    w_query,
    key_weight,
    value_weight,
):
    tok_rows = query.shape[0]
    kv_local = key_projected.shape[1] // HEAD_SIZE
    heads_local = kv_local * GROUP
    kv_cols = kv_local * HEAD_SIZE
    q_start = lax.axis_index("ctx") * tok_rows
    cosine, sine = rope_tables(positions, HEAD_SIZE)
    key_three = key_projected.astype(jnp.float32).reshape(tok_rows, kv_local, HEAD_SIZE)
    key_rotated = (
        (key_three * cosine[:, None, :] + swap_halves(key_three) * sine[:, None, :])
        .astype(jnp.bfloat16)
        .reshape(tok_rows, kv_cols)
    )
    delta = jnp.sum(
        (output_gradient.astype(jnp.float32) * attention_output.astype(jnp.float32)).reshape(
            tok_rows, heads_local, HEAD_SIZE
        ),
        -1,
    ).T
    kv_whole = lax.all_gather(
        jnp.concatenate([key_rotated, value], 1), "ctx", axis=0, tiled=True
    )
    seg_row = lax.dynamic_slice_in_dim(segments, q_start, tok_rows).reshape(1, tok_rows)
    first_tile = (q_start // TILE).astype(jnp.int32).reshape(1)
    query_grad, terms = attention(
        first_tile, block_mask, query, output_gradient, lse, delta, cosine, sine, kv_whole, seg_row
    )
    summed = lax.psum_scatter(terms, "ctx", scatter_dimension=0, tiled=True)
    key_three = (summed[:, :kv_cols] * SCALE).reshape(tok_rows, kv_local, HEAD_SIZE)
    key_gradient = (key_three * cosine[:, None, :] - swap_halves(key_three) * sine[:, None, :]).reshape(
        tok_rows, kv_cols
    )
    dkv = jnp.concatenate([key_gradient, summed[:, kv_cols:]], 1).astype(jnp.bfloat16)
    return project(n_tp, query_grad, dkv, w_query, key_weight, value_weight)


def solution(mesh):
    in_specs = (
        P("ctx", "tp"),
        P("ctx", "tp"),
        P("ctx", "tp"),
        P("ctx", "tp"),
        P("ctx", "tp"),
        P("tp", "ctx"),
        P(),
        P("ctx"),
        P(),
        P(None, "tp"),
        P(None, "tp"),
        P(None, "tp"),
    )
    out_specs = P("tp", "ctx")
    body = functools.partial(local, mesh.shape["ctx"], mesh.shape["tp"])
    return jax.shard_map(body, mesh=mesh, in_specs=in_specs, out_specs=out_specs, check_vma=False)
```

```python
import functools

import jax
import jax.numpy as jnp
from jax import lax
from jax.experimental import pallas as pl
from jax.experimental.pallas import tpu as pltpu
from jax.sharding import PartitionSpec as P

QUERY_HEADS = 40
KEY_VALUE_HEADS = 8
HEAD_SIZE = 128
TILE = 128
GROUP = QUERY_HEADS // KEY_VALUE_HEADS
SCALE = HEAD_SIZE ** (-0.5)
MESH = pl.DeviceIdType.MESH
VMEM_BYTES = 56 * 1024 * 1024
ATTENTION_BYTES = 24 * 1024 * 1024

rope_base = 1000000.0


def rope_tables(positions, head_dim):
    half = head_dim // 2
    exponent = jnp.arange(half).astype(jnp.float32) * (2.0 / head_dim)
    inverse = jnp.power(jnp.float32(rope_base), -exponent)
    angles = positions.astype(jnp.float32)[:, None] * inverse[None, :]
    cosine_table = jnp.cos(angles)
    sine_table = jnp.sin(angles)
    return (
        jnp.concatenate([cosine_table, cosine_table], 1),
        jnp.concatenate([-sine_table, sine_table], 1),
    )


def dot(a, b, dims=((1,), (0,))):
    return lax.dot_general(a, b, (dims, ((), ())), preferred_element_type=jnp.float32)


def gather_kernel(
    n, kp_ref, v_ref, q_ref, do_ref, ao_ref, cos_ref, sin_ref,
    kv_ref, qs_ref, dos_ref, qt_ref, dot_ref, delta_ref,
    send_sem, recv_sem, pass_sem, pass_recv_sem,
):
    me = lax.axis_index("ctx")
    chip, core = me // 2, lax.rem(me, 2)
    sibling = 2 * chip + 1 - core
    chips = n // 2
    tokens, kv_cols = kp_ref.shape
    heads = q_ref.shape[1] // HEAD_SIZE
    q_tiles = tokens // TILE

    barrier = pltpu.get_barrier_semaphore()
    for away in range(1, chips):
        other = 2 * lax.rem(chip + away, chips) + core
        pl.semaphore_signal(barrier, inc=1, device_id={"ctx": other}, device_id_type=MESH)
    pl.semaphore_signal(barrier, inc=1, device_id={"ctx": sibling}, device_id_type=MESH)

    for c in range(kv_cols // HEAD_SIZE):
        cols = slice(c * HEAD_SIZE, (c + 1) * HEAD_SIZE)
        x = kp_ref[:, cols].astype(jnp.float32)
        x = x * cos_ref[...] + pltpu.roll(x, HEAD_SIZE // 2, 1) * sin_ref[...]
        kv_ref[me, :, cols] = x.astype(jnp.bfloat16)
    kv_ref[me, :, kv_cols:] = v_ref[...]

    def direct(source, target):
        slot = 2 * source + core
        return pltpu.make_async_remote_copy(
            src_ref=kv_ref.at[slot],
            dst_ref=kv_ref.at[slot],
            send_sem=send_sem.at[target],
            recv_sem=recv_sem.at[source],
            device_id={"ctx": 2 * target + core},
            device_id_type=MESH,
        )

    def handed(source, from_core):
        slot = 2 * source + from_core
        return pltpu.make_async_remote_copy(
            src_ref=kv_ref.at[slot],
            dst_ref=kv_ref.at[slot],
            send_sem=pass_sem.at[source],
            recv_sem=pass_recv_sem.at[source],
            device_id={"ctx": sibling},
            device_id_type=MESH,
        )

    pl.semaphore_wait(barrier, chips)
    for away in range(chips - 1, 0, -1):

        @pl.when(chip + away < chips)
        def _():
            direct(chip, jnp.minimum(chip + away, chips - 1)).start()

    handed(chip, core).start()

    @pl.loop(0, q_tiles * heads)
    def _(i):
        t, h = i // heads, lax.rem(i, heads)
        c, g = h // GROUP, lax.rem(h, GROUP)
        rows = pl.ds(pl.multiple_of(t * TILE, TILE), TILE)
        cols = pl.ds(pl.multiple_of(h * HEAD_SIZE, HEAD_SIZE), HEAD_SIZE)
        part = pl.ds(pl.multiple_of(g * TILE, TILE), TILE)
        x = q_ref[rows, cols].astype(jnp.float32)
        x = x * cos_ref[rows, :] + pltpu.roll(x, HEAD_SIZE // 2, 1) * sin_ref[rows, :]
        xb = x.astype(jnp.bfloat16)
        qs_ref[t, c, part, :] = xb
        qt_ref[t, c, :, part] = xb.astype(jnp.float32).T.astype(jnp.bfloat16)
        y = do_ref[rows, cols]
        dos_ref[t, c, part, :] = y
        y_turned = y.astype(jnp.float32).T
        dot_ref[t, c, :, part] = y_turned.astype(jnp.bfloat16)
        o_turned = ao_ref[rows, cols].astype(jnp.float32).T
        delta_ref[t, c, :, part] = jnp.sum(y_turned * o_turned, axis=0, keepdims=True)

    for away in range(1, chips):

        @pl.when(chip - away >= 0)
        def _():
            source = jnp.maximum(chip - away, 0)
            direct(source, chip).wait_recv()
            handed(source, core).start()

    for away in range(chips):

        @pl.when(chip - away >= 0)
        def _():
            source = jnp.maximum(chip - away, 0)
            handed(source, 1 - core).wait_recv()
            handed(source, core).wait_send()

    for away in range(1, chips):

        @pl.when(chip + away < chips)
        def _():
            direct(chip, jnp.minimum(chip + away, chips - 1)).wait_send()


def gather(n, key_projected, value, query, grad, attention_output, cosine, sine):
    tokens, kv_cols = key_projected.shape
    kv_local = kv_cols // HEAD_SIZE
    q_tiles = tokens // TILE
    wide = GROUP * TILE
    vm = pl.BlockSpec(memory_space=pltpu.VMEM)
    dma = pltpu.SemaphoreType.DMA
    stacked = jax.ShapeDtypeStruct((q_tiles, kv_local, wide, HEAD_SIZE), jnp.bfloat16)
    turned = jax.ShapeDtypeStruct((q_tiles, kv_local, HEAD_SIZE, wide), jnp.bfloat16)
    return pl.pallas_call(
        functools.partial(gather_kernel, n),
        out_shape=(
            jax.ShapeDtypeStruct((n, tokens, 2 * kv_cols), jnp.bfloat16),
            stacked,
            stacked,
            turned,
            turned,
            jax.ShapeDtypeStruct((q_tiles, kv_local, 1, wide), jnp.float32),
        ),
        in_specs=[vm] * 7,
        out_specs=(vm,) * 6,
        scratch_shapes=[dma((n // 2,))] * 4,
        compiler_params=pltpu.CompilerParams(
            collective_id=1, has_side_effects=True, vmem_limit_bytes=ATTENTION_BYTES
        ),
        name="gather",
    )(key_projected, value, query, grad, attention_output, cosine, sine)


def attention_kernel(
    start_ref, mask_ref, qs, dos, qt_s, dot_s, lse_ref, delta_s, cos_ref, sin_ref, kv_ref, segq_ref, segk_ref,
    dq_ref, dkv_ref, lse_s, dqt,
):
    tokens = dq_ref.shape[0]
    kv_local = kv_ref.shape[1] // (2 * HEAD_SIZE)
    q_tiles = tokens // TILE
    first_tile = start_ref[0]
    dkv_ref[...] = jnp.zeros_like(dkv_ref)
    dqt[...] = jnp.zeros_like(dqt)
    for t in range(q_tiles):
        for h in range(kv_local * GROUP):
            c, g = h // GROUP, h % GROUP
            lse_s[t, c, :, g * TILE : (g + 1) * TILE] = lse_ref[h : h + 1, t * TILE : (t + 1) * TILE]

    def pair(t, k_tile, allowed):
        k_rows = pl.ds(pl.multiple_of(k_tile * TILE, TILE), TILE)
        for c in range(kv_local):
            key_cols = slice(c * HEAD_SIZE, (c + 1) * HEAD_SIZE)
            val_cols = slice((kv_local + c) * HEAD_SIZE, (kv_local + c + 1) * HEAD_SIZE)
            k = kv_ref[k_rows, key_cols]
            v = kv_ref[k_rows, val_cols]
            scores = dot(k, qt_s[t, c]) * SCALE
            probs = jnp.exp(scores - lse_s[t, c])
            if allowed is not None:
                probs = jnp.where(allowed, probs, 0.0)
            dscore = probs * (dot(v, dot_s[t, c]) - delta_s[t, c])
            pb = probs.astype(jnp.bfloat16)
            db = dscore.astype(jnp.bfloat16)
            dkv_ref[k_rows, key_cols] += dot(db, qs[t, c])
            dkv_ref[k_rows, val_cols] += dot(pb, dos[t, c])
            kt = k.astype(jnp.float32).T.astype(jnp.bfloat16)
            dqt[t, c] += dot(kt, db)

    for t in range(q_tiles):
        own = first_tile + t

        @pl.loop(0, own)
        def _(k_tile):
            @pl.when(mask_ref[own, k_tile] > 0)
            def _():
                pair(t, k_tile, None)

        row = lax.broadcasted_iota(jnp.int32, (TILE, TILE), 0)
        col = lax.broadcasted_iota(jnp.int32, (TILE, TILE), 1)
        seg_k = segk_ref[t * TILE : (t + 1) * TILE, :]
        seg_q = segq_ref[:, t * TILE : (t + 1) * TILE]
        inner = jnp.where((row <= col) & (seg_k == seg_q), 1.0, 0.0)
        inner = jnp.concatenate([inner] * GROUP, 1) > 0.5
        pair(t, own, inner)

        rows = slice(t * TILE, (t + 1) * TILE)
        cosine = cos_ref[rows, :]
        sine = sin_ref[rows, :]
        for h in range(kv_local * GROUP):
            c, g = h // GROUP, h % GROUP
            x = (dqt[t, c, :, g * TILE : (g + 1) * TILE] * SCALE).T
            x = x * cosine - pltpu.roll(x, HEAD_SIZE // 2, 1) * sine
            dq_ref[rows, h * HEAD_SIZE : (h + 1) * HEAD_SIZE] = x.astype(jnp.bfloat16)


def attention(first_tile, block_mask, prepared, lse, cosine, sine, kv_whole, seg_row):
    qs, dos, turned_q, turned_do, delta = prepared
    q_tiles, kv_local, wide, _ = qs.shape
    tokens = q_tiles * TILE
    vm = pl.BlockSpec(memory_space=pltpu.VMEM)
    sm = pl.BlockSpec(memory_space=pltpu.SMEM)
    return pl.pallas_call(
        attention_kernel,
        out_shape=(
            jax.ShapeDtypeStruct((tokens, kv_local * GROUP * HEAD_SIZE), jnp.bfloat16),
            jax.ShapeDtypeStruct(kv_whole.shape, jnp.float32),
        ),
        in_specs=[sm, sm] + [vm] * 11,
        out_specs=(vm, vm),
        scratch_shapes=[
            pltpu.VMEM((q_tiles, kv_local, 1, wide), jnp.float32),
            pltpu.VMEM((q_tiles, kv_local, HEAD_SIZE, wide), jnp.float32),
        ],
        compiler_params=pltpu.CompilerParams(vmem_limit_bytes=ATTENTION_BYTES),
        name="attention",
    )(
        first_tile, block_mask, qs, dos, turned_q, turned_do, lse, delta, cosine, sine, kv_whole,
        seg_row, seg_row.reshape(tokens, 1),
    )


def project_kernel(
    n_ctx, n, dq_ref, terms_ref, cos_ref, sin_ref, wq_ref, wk_ref, wv_ref, out_ref,
    wq, wk, wv, acc, send, send_scale, recv, recv_scale,
    dkv_ref, total, near, part, part_scale, far, far_scale,
    w_sem, send_sem, recv_sem, send_scale_sem, recv_scale_sem,
    near_send_sem, near_sem, part_sem, far_sem, part_scale_sem, far_scale_sem,
):
    me = lax.axis_index("tp")
    chips = n_ctx // 2
    place = lax.axis_index("ctx")
    chip, core = place // 2, lax.rem(place, 2)
    sibling = 2 * chip + 1 - core
    tokens, kv_width = dkv_ref.shape
    kv_half = kv_width // 2
    group = tokens // 8
    chunk_rows = out_ref.shape[0]
    sub_rows = acc.shape[0]
    subs = chunk_rows // sub_rows
    steps = 2 * (n - 1) * subs

    def plan(i):
        way = lax.rem(i, 2)
        rightward = jnp.where(me < n // 2, 1 - way, way)
        sub = lax.rem(i // 2, subs)
        step = i // (2 * subs)
        chunk = jnp.where(rightward == 1, n - 1 - step, step)
        active = jnp.where(rightward == 1, chunk > me, chunk < me)
        return rightward, chunk, sub, active

    def weight_copies(chunk, sub):
        at = chunk * subs + sub
        rows = pl.ds(pl.multiple_of(at * sub_rows, sub_rows), sub_rows)
        return [
            pltpu.make_async_copy(src.at[rows, :], dst.at[rows, :], w_sem.at[j, at])
            for j, (src, dst) in enumerate(((wq_ref, wq), (wk_ref, wk), (wv_ref, wv)))
        ]

    def remote(rightward, chunk, sub):
        slot = chunk * subs + sub
        to = jnp.where(rightward == 1, jnp.minimum(me + 1, n - 1), jnp.maximum(me - 1, 0))
        return [
            pltpu.make_async_remote_copy(
                src_ref=s.at[slot],
                dst_ref=r.at[rightward, slot],
                send_sem=ss.at[slot],
                recv_sem=rs.at[rightward, slot],
                device_id={"tp": to},
                device_id_type=MESH,
            )
            for s, r, ss, rs in (
                (send, recv, send_sem, recv_sem),
                (send_scale, recv_scale, send_scale_sem, recv_scale_sem),
            )
        ]

    def own_term(chunk, sub):
        for copy in weight_copies(chunk, sub):
            copy.wait()
        at = chunk * subs + sub
        rows = pl.ds(pl.multiple_of(at * sub_rows, sub_rows), sub_rows)
        half = wk.shape[1]
        contract = ((1,), (1,))
        total = dot(wq[rows, :], dq_ref[...], contract)
        total = total + dot(wk[rows, :], dkv_ref[:, :half], contract)
        acc[...] = total + dot(wv[rows, :], dkv_ref[:, half:], contract)

    def add_received(rightward, chunk, sub):
        for copy in remote(rightward, chunk, sub):
            copy.wait_recv()
        slot = chunk * subs + sub
        scale = recv_scale[rightward, slot, 0:1, :]
        acc[...] += recv[rightward, slot].astype(jnp.int32).astype(jnp.float32) * scale

    @pl.loop(0, steps)
    def _(i):
        _, chunk, sub, active = plan(i)

        @pl.when(active)
        def _():
            for copy in weight_copies(chunk, sub):
                copy.start()

    @pl.loop(0, subs)
    def _(sub):
        for copy in weight_copies(me, sub):
            copy.start()

    barrier = pltpu.get_barrier_semaphore()

    @pl.when(me > 0)
    def _():
        pl.semaphore_signal(barrier, inc=1, device_id={"tp": jnp.maximum(me - 1, 0)}, device_id_type=MESH)

    @pl.when(me < n - 1)
    def _():
        pl.semaphore_signal(barrier, inc=1, device_id={"tp": jnp.minimum(me + 1, n - 1)}, device_id_type=MESH)

    for away in range(1, chips):
        other = 2 * lax.rem(chip + away, chips) + core
        pl.semaphore_signal(barrier, inc=1, device_id={"ctx": other}, device_id_type=MESH)
    pl.semaphore_signal(barrier, inc=1, device_id={"ctx": sibling}, device_id_type=MESH)
    peers = jnp.where(me > 0, 1, 0) + jnp.where(me < n - 1, 1, 0) + chips
    pl.semaphore_wait(barrier, peers)

    def token_rows(block):
        return pl.ds(pl.multiple_of(block * tokens, tokens), tokens)

    def to_sibling(j):
        return pltpu.make_async_remote_copy(
            src_ref=terms_ref.at[token_rows(2 * j + 1 - core), :],
            dst_ref=near.at[j],
            send_sem=near_send_sem.at[j],
            recv_sem=near_sem.at[j],
            device_id={"ctx": sibling},
            device_id_type=MESH,
        )

    def to_owner(source, j):
        return [
            pltpu.make_async_remote_copy(
                src_ref=p.at[j],
                dst_ref=f.at[source],
                send_sem=ps.at[j],
                recv_sem=fs.at[source],
                device_id={"ctx": 2 * j + core},
                device_id_type=MESH,
            )
            for p, f, ps, fs in (
                (part, far, part_sem, far_sem),
                (part_scale, far_scale, part_scale_sem, far_scale_sem),
            )
        ]

    @pl.loop(0, chip + 1)
    def _(j):
        to_sibling(j).start()

    @pl.loop(0, chip)
    def _(j):
        to_sibling(j).wait_recv()
        for r in range(8):
            rows = slice(r * group, (r + 1) * group)
            at = pl.ds(pl.multiple_of((2 * j + core) * tokens + r * group, group), group)
            x = terms_ref[at, :] + near[j, rows, :]
            largest = jnp.maximum(jnp.max(jnp.abs(x), axis=0, keepdims=True), 1e-30)
            part_scale[j, r : r + 1, :] = largest * (1.0 / 32767.0)
            part[j, rows, :] = jnp.round(x * (32767.0 / largest)).astype(jnp.int32).astype(jnp.int16)
        for copy in to_owner(chip, j):
            copy.start()

    to_sibling(chip).wait_recv()
    total[...] = terms_ref[token_rows(place), :] + near[chip]

    @pl.loop(chip + 1, chips)
    def _(j):
        for copy in to_owner(j, chip):
            copy.wait_recv()
        for r in range(8):
            rows = slice(r * group, (r + 1) * group)
            x = far[j, rows, :].astype(jnp.int32).astype(jnp.float32)
            total[rows, :] += x * far_scale[j, r : r + 1, :]

    for c in range(kv_half // HEAD_SIZE):
        cols = slice(c * HEAD_SIZE, (c + 1) * HEAD_SIZE)
        x = total[:, cols] * SCALE
        x = x * cos_ref[...] - pltpu.roll(x, HEAD_SIZE // 2, 1) * sin_ref[...]
        dkv_ref[:, cols] = x.astype(jnp.bfloat16)
    dkv_ref[:, kv_half:] = total[:, kv_half:].astype(jnp.bfloat16)

    @pl.loop(0, chip + 1)
    def _(j):
        to_sibling(j).wait_send()

    @pl.loop(0, chip)
    def _(j):
        for copy in to_owner(chip, j):
            copy.wait_send()

    @pl.loop(0, steps)
    def _(i):
        rightward, chunk, sub, active = plan(i)

        @pl.when(active)
        def _():
            own_term(chunk, sub)

            @pl.when(jnp.where(rightward == 1, me > 0, me < n - 1))
            def _():
                add_received(rightward, chunk, sub)

            slot = chunk * subs + sub
            largest = jnp.maximum(jnp.max(jnp.abs(acc[...]), axis=0, keepdims=True), 1e-30)
            send_scale[slot] = jnp.broadcast_to(largest * (1.0 / 32767.0), send_scale.shape[1:])
            coded = jnp.round(acc[...] * (32767.0 / largest))
            send[slot] = coded.astype(jnp.int32).astype(jnp.int16)
            for copy in remote(rightward, chunk, sub):
                copy.start()

    @pl.loop(0, subs)
    def _(sub):
        own_term(me, sub)

        @pl.when(me > 0)
        def _():
            add_received(1, me, sub)

        @pl.when(me < n - 1)
        def _():
            add_received(0, me, sub)

        rows = pl.ds(pl.multiple_of(sub * sub_rows, sub_rows), sub_rows)
        out_ref[rows, :] = acc[...].astype(jnp.bfloat16)

    @pl.loop(0, steps)
    def _(i):
        rightward, chunk, sub, active = plan(i)

        @pl.when(active)
        def _():
            for copy in remote(rightward, chunk, sub):
                copy.wait_send()


def project(n_ctx, n, dq, terms, cosine, sine, w_query, key_weight, value_weight):
    tokens = dq.shape[0]
    kv_width = terms.shape[1]
    chips = n_ctx // 2
    width = w_query.shape[0]
    chunk_rows = width // n
    sub_rows = 320 if chunk_rows % 320 == 0 else chunk_rows
    slots = width // sub_rows
    vm = pl.BlockSpec(memory_space=pltpu.VMEM)
    hbm = pl.BlockSpec(memory_space=pl.ANY)
    dma = pltpu.SemaphoreType.DMA
    return pl.pallas_call(
        functools.partial(project_kernel, n_ctx, n),
        out_shape=jax.ShapeDtypeStruct((chunk_rows, tokens), jnp.bfloat16),
        in_specs=[vm, vm, vm, vm, hbm, hbm, hbm],
        out_specs=vm,
        scratch_shapes=[
            pltpu.VMEM(w_query.shape, jnp.bfloat16),
            pltpu.VMEM(key_weight.shape, jnp.bfloat16),
            pltpu.VMEM(value_weight.shape, jnp.bfloat16),
            pltpu.VMEM((sub_rows, tokens), jnp.float32),
            pltpu.VMEM((slots, sub_rows, tokens), jnp.int16),
            pltpu.VMEM((slots, 8, tokens), jnp.float32),
            pltpu.VMEM((2, slots, sub_rows, tokens), jnp.int16),
            pltpu.VMEM((2, slots, 8, tokens), jnp.float32),
            pltpu.VMEM((tokens, kv_width), jnp.bfloat16),
            pltpu.VMEM((tokens, kv_width), jnp.float32),
            pltpu.VMEM((chips, tokens, kv_width), jnp.float32),
            pltpu.VMEM((chips, tokens, kv_width), jnp.int16),
            pltpu.VMEM((chips, 8, kv_width), jnp.float32),
            pltpu.VMEM((chips, tokens, kv_width), jnp.int16),
            pltpu.VMEM((chips, 8, kv_width), jnp.float32),
            dma((3, slots)),
            dma((slots,)),
            dma((2, slots)),
            dma((slots,)),
            dma((2, slots)),
        ]
        + [dma((chips,))] * 6,
        compiler_params=pltpu.CompilerParams(
            collective_id=2, has_side_effects=True, vmem_limit_bytes=VMEM_BYTES
        ),
        name="project",
    )(dq, terms, cosine, sine, w_query, key_weight, value_weight)


def local(
    n_ctx,
    n_tp,
    query,
    key_projected,
    value,
    attention_output,
    output_gradient,
    lse,
    block_mask,
    positions,
    segments,
    w_query,
    key_weight,
    value_weight,
):
    tok_rows = query.shape[0]
    q_start = lax.axis_index("ctx") * tok_rows
    cosine, sine = rope_tables(positions, HEAD_SIZE)
    kv_blocks, *prepared = gather(
        n_ctx, key_projected, value, query, output_gradient, attention_output, cosine, sine
    )
    kv_whole = kv_blocks.reshape(n_ctx * tok_rows, kv_blocks.shape[-1])
    seg_row = lax.dynamic_slice_in_dim(segments, q_start, tok_rows).reshape(1, tok_rows)
    first_tile = (q_start // TILE).astype(jnp.int32).reshape(1)
    query_grad, terms = attention(
        first_tile, block_mask, prepared, lse, cosine, sine, kv_whole, seg_row
    )
    return project(n_ctx, n_tp, query_grad, terms, cosine, sine, w_query, key_weight, value_weight)


def solution(mesh):
    in_specs = (
        P("ctx", "tp"),
        P("ctx", "tp"),
        P("ctx", "tp"),
        P("ctx", "tp"),
        P("ctx", "tp"),
        P("tp", "ctx"),
        P(),
        P("ctx"),
        P(),
        P(None, "tp"),
        P(None, "tp"),
        P(None, "tp"),
    )
    out_specs = P("tp", "ctx")
    body = functools.partial(local, mesh.shape["ctx"], mesh.shape["tp"])
    return jax.shard_map(body, mesh=mesh, in_specs=in_specs, out_specs=out_specs, check_vma=False)
```

```python
import functools

import jax
import jax.numpy as jnp
from jax import lax
from jax.experimental import pallas as pl
from jax.experimental.pallas import tpu as pltpu
from jax.sharding import PartitionSpec as P

QUERY_HEADS = 40
KEY_VALUE_HEADS = 8
HEAD_SIZE = 128
TILE = 128
GROUP = QUERY_HEADS // KEY_VALUE_HEADS
SCALE = HEAD_SIZE ** (-0.5)
MESH = pl.DeviceIdType.MESH
VMEM_BYTES = 56 * 1024 * 1024
ATTENTION_BYTES = 24 * 1024 * 1024

rope_base = 1000000.0


def rope_tables(positions, head_dim):
    half = head_dim // 2
    exponent = jnp.arange(half).astype(jnp.float32) * (2.0 / head_dim)
    inverse = jnp.power(jnp.float32(rope_base), -exponent)
    angles = positions.astype(jnp.float32)[:, None] * inverse[None, :]
    cosine_table = jnp.cos(angles)
    sine_table = jnp.sin(angles)
    return (
        jnp.concatenate([cosine_table, cosine_table], 1),
        jnp.concatenate([-sine_table, sine_table], 1),
    )


def dot(a, b, dims=((1,), (0,))):
    return lax.dot_general(a, b, (dims, ((), ())), preferred_element_type=jnp.float32)


def gather_kernel(
    n, kp_ref, v_ref, q_hbm, do_hbm, ao_hbm, cos_ref, sin_ref,
    kv_ref, qs_ref, dos_ref, qt_ref, dot_ref, delta_ref,
    q_ref, do_ref, ao_ref, load_sem, send_sem, recv_sem, pass_sem, pass_recv_sem,
):
    loads = [
        pltpu.make_async_copy(src, dst, load_sem.at[j])
        for j, (src, dst) in enumerate(((q_hbm, q_ref), (do_hbm, do_ref), (ao_hbm, ao_ref)))
    ]
    for copy in loads:
        copy.start()
    me = lax.axis_index("ctx")
    chip, core = me // 2, lax.rem(me, 2)
    sibling = 2 * chip + 1 - core
    chips = n // 2
    tokens, kv_cols = kp_ref.shape
    heads = q_ref.shape[1] // HEAD_SIZE
    q_tiles = tokens // TILE

    barrier = pltpu.get_barrier_semaphore()
    for away in range(1, chips):
        other = 2 * lax.rem(chip + away, chips) + core
        pl.semaphore_signal(barrier, inc=1, device_id={"ctx": other}, device_id_type=MESH)
    pl.semaphore_signal(barrier, inc=1, device_id={"ctx": sibling}, device_id_type=MESH)

    for c in range(kv_cols // HEAD_SIZE):
        cols = slice(c * HEAD_SIZE, (c + 1) * HEAD_SIZE)
        x = kp_ref[:, cols].astype(jnp.float32)
        x = x * cos_ref[...] + pltpu.roll(x, HEAD_SIZE // 2, 1) * sin_ref[...]
        kv_ref[me, :, cols] = x.astype(jnp.bfloat16)
    kv_ref[me, :, kv_cols:] = v_ref[...]

    def direct(source, target):
        slot = 2 * source + core
        return pltpu.make_async_remote_copy(
            src_ref=kv_ref.at[slot],
            dst_ref=kv_ref.at[slot],
            send_sem=send_sem.at[target],
            recv_sem=recv_sem.at[source],
            device_id={"ctx": 2 * target + core},
            device_id_type=MESH,
        )

    def handed(source, from_core):
        slot = 2 * source + from_core
        return pltpu.make_async_remote_copy(
            src_ref=kv_ref.at[slot],
            dst_ref=kv_ref.at[slot],
            send_sem=pass_sem.at[source],
            recv_sem=pass_recv_sem.at[source],
            device_id={"ctx": sibling},
            device_id_type=MESH,
        )

    pl.semaphore_wait(barrier, chips)
    for away in range(chips - 1, 0, -1):

        @pl.when(chip + away < chips)
        def _():
            direct(chip, jnp.minimum(chip + away, chips - 1)).start()

    handed(chip, core).start()
    for copy in loads:
        copy.wait()

    @pl.loop(0, q_tiles * heads)
    def _(i):
        t, h = i // heads, lax.rem(i, heads)
        c, g = h // GROUP, lax.rem(h, GROUP)
        rows = pl.ds(pl.multiple_of(t * TILE, TILE), TILE)
        cols = pl.ds(pl.multiple_of(h * HEAD_SIZE, HEAD_SIZE), HEAD_SIZE)
        part = pl.ds(pl.multiple_of(g * TILE, TILE), TILE)
        x = q_ref[rows, cols].astype(jnp.float32)
        x = x * cos_ref[rows, :] + pltpu.roll(x, HEAD_SIZE // 2, 1) * sin_ref[rows, :]
        xb = x.astype(jnp.bfloat16)
        qs_ref[t, c, part, :] = xb
        qt_ref[t, c, :, part] = xb.astype(jnp.float32).T.astype(jnp.bfloat16)
        y = do_ref[rows, cols]
        dos_ref[t, c, part, :] = y
        y_turned = y.astype(jnp.float32).T
        dot_ref[t, c, :, part] = y_turned.astype(jnp.bfloat16)
        o_turned = ao_ref[rows, cols].astype(jnp.float32).T
        delta_ref[t, c, :, part] = jnp.sum(y_turned * o_turned, axis=0, keepdims=True)

    for away in range(1, chips):

        @pl.when(chip - away >= 0)
        def _():
            source = jnp.maximum(chip - away, 0)
            direct(source, chip).wait_recv()
            handed(source, core).start()

    for away in range(chips):

        @pl.when(chip - away >= 0)
        def _():
            source = jnp.maximum(chip - away, 0)
            handed(source, 1 - core).wait_recv()
            handed(source, core).wait_send()

    for away in range(1, chips):

        @pl.when(chip + away < chips)
        def _():
            direct(chip, jnp.minimum(chip + away, chips - 1)).wait_send()


def gather(n, key_projected, value, query, grad, attention_output, cosine, sine):
    tokens, kv_cols = key_projected.shape
    kv_local = kv_cols // HEAD_SIZE
    q_tiles = tokens // TILE
    wide = GROUP * TILE
    vm = pl.BlockSpec(memory_space=pltpu.VMEM)
    hbm = pl.BlockSpec(memory_space=pl.ANY)
    dma = pltpu.SemaphoreType.DMA
    stacked = jax.ShapeDtypeStruct((q_tiles, kv_local, wide, HEAD_SIZE), jnp.bfloat16)
    turned = jax.ShapeDtypeStruct((q_tiles, kv_local, HEAD_SIZE, wide), jnp.bfloat16)
    return pl.pallas_call(
        functools.partial(gather_kernel, n),
        out_shape=(
            jax.ShapeDtypeStruct((n, tokens, 2 * kv_cols), jnp.bfloat16),
            stacked,
            stacked,
            turned,
            turned,
            jax.ShapeDtypeStruct((q_tiles, kv_local, 1, wide), jnp.float32),
        ),
        in_specs=[vm, vm, hbm, hbm, hbm, vm, vm],
        out_specs=(vm,) * 6,
        scratch_shapes=[pltpu.VMEM(query.shape, jnp.bfloat16)] * 3 + [dma((3,))] + [dma((n // 2,))] * 4,
        compiler_params=pltpu.CompilerParams(
            collective_id=1, has_side_effects=True, vmem_limit_bytes=ATTENTION_BYTES
        ),
        name="gather",
    )(key_projected, value, query, grad, attention_output, cosine, sine)


def attention_kernel(
    start_ref, mask_ref, qs, dos, qt_s, dot_s, lse_ref, delta_s, cos_ref, sin_ref, kv_ref, segq_ref, segk_ref,
    dq_ref, dkv_ref, lse_s, dqt, needed_ref,
):
    tokens = dq_ref.shape[0]
    kv_local = kv_ref.shape[1] // (2 * HEAD_SIZE)
    q_tiles = tokens // TILE
    first_tile = start_ref[0]
    dkv_ref[...] = jnp.zeros_like(dkv_ref)
    dqt[...] = jnp.zeros_like(dqt)
    for t in range(q_tiles):
        for h in range(kv_local * GROUP):
            c, g = h // GROUP, h % GROUP
            lse_s[t, c, :, g * TILE : (g + 1) * TILE] = lse_ref[h : h + 1, t * TILE : (t + 1) * TILE]

    def terms(t, k_tiles, allowed):
        spans = [pl.ds(pl.multiple_of(k * TILE, TILE), TILE) for k in k_tiles]
        for c in range(kv_local):
            key_cols = slice(c * HEAD_SIZE, (c + 1) * HEAD_SIZE)
            val_cols = slice((kv_local + c) * HEAD_SIZE, (kv_local + c + 1) * HEAD_SIZE)
            k = jnp.concatenate([kv_ref[span, key_cols] for span in spans], 0)
            v = jnp.concatenate([kv_ref[span, val_cols] for span in spans], 0)
            scores = dot(k, qt_s[t, c]) * SCALE
            probs = jnp.exp(scores - lse_s[t, c])
            if allowed is not None:
                probs = jnp.where(allowed, probs, 0.0)
            dscore = probs * (dot(v, dot_s[t, c]) - delta_s[t, c])
            pb = probs.astype(jnp.bfloat16)
            db = dscore.astype(jnp.bfloat16)
            dk = dot(db, qs[t, c])
            dv = dot(pb, dos[t, c])
            for j, span in enumerate(spans):
                dkv_ref[span, key_cols] += dk[j * TILE : (j + 1) * TILE]
                dkv_ref[span, val_cols] += dv[j * TILE : (j + 1) * TILE]
            kt = k.astype(jnp.float32).T.astype(jnp.bfloat16)
            dqt[t, c] += dot(kt, db)

    for t in range(q_tiles):
        own = first_tile + t

        def note(k_tile, count):
            needed_ref[count] = k_tile
            return count + jnp.where(mask_ref[own, k_tile] > 0, 1, 0)

        count = lax.fori_loop(0, own, note, jnp.int32(0))

        @pl.loop(0, count // 2)
        def _(i):
            terms(t, (needed_ref[2 * i], needed_ref[2 * i + 1]), None)

        row = lax.broadcasted_iota(jnp.int32, (TILE, TILE), 0)
        col = lax.broadcasted_iota(jnp.int32, (TILE, TILE), 1)
        seg_k = segk_ref[t * TILE : (t + 1) * TILE, :]
        seg_q = segq_ref[:, t * TILE : (t + 1) * TILE]
        inner = jnp.where((row <= col) & (seg_k == seg_q), 1.0, 0.0)
        inner = jnp.concatenate([inner] * GROUP, 1)

        @pl.when(lax.rem(count, 2) == 1)
        def _():
            whole = jnp.concatenate([jnp.ones_like(inner), inner], 0)
            terms(t, (needed_ref[count - 1], own), whole > 0.5)

        @pl.when(lax.rem(count, 2) == 0)
        def _():
            terms(t, (own,), inner > 0.5)

        rows = slice(t * TILE, (t + 1) * TILE)
        cosine = cos_ref[rows, :]
        sine = sin_ref[rows, :]
        for h in range(kv_local * GROUP):
            c, g = h // GROUP, h % GROUP
            x = (dqt[t, c, :, g * TILE : (g + 1) * TILE] * SCALE).T
            x = x * cosine - pltpu.roll(x, HEAD_SIZE // 2, 1) * sine
            dq_ref[rows, h * HEAD_SIZE : (h + 1) * HEAD_SIZE] = x.astype(jnp.bfloat16)


def attention(first_tile, block_mask, prepared, lse, cosine, sine, kv_whole, seg_row):
    qs, dos, turned_q, turned_do, delta = prepared
    q_tiles, kv_local, wide, _ = qs.shape
    tokens = q_tiles * TILE
    vm = pl.BlockSpec(memory_space=pltpu.VMEM)
    sm = pl.BlockSpec(memory_space=pltpu.SMEM)
    return pl.pallas_call(
        attention_kernel,
        out_shape=(
            jax.ShapeDtypeStruct((tokens, kv_local * GROUP * HEAD_SIZE), jnp.bfloat16),
            jax.ShapeDtypeStruct(kv_whole.shape, jnp.float32),
        ),
        in_specs=[sm, sm] + [vm] * 11,
        out_specs=(vm, vm),
        scratch_shapes=[
            pltpu.VMEM((q_tiles, kv_local, 1, wide), jnp.float32),
            pltpu.VMEM((q_tiles, kv_local, HEAD_SIZE, wide), jnp.float32),
            pltpu.SMEM((block_mask.shape[0],), jnp.int32),
        ],
        compiler_params=pltpu.CompilerParams(vmem_limit_bytes=ATTENTION_BYTES),
        name="attention",
    )(
        first_tile, block_mask, qs, dos, turned_q, turned_do, lse, delta, cosine, sine, kv_whole,
        seg_row, seg_row.reshape(tokens, 1),
    )


def project_kernel(
    n_ctx, n, dq_hbm, terms_ref, cos_ref, sin_ref, wq_ref, wk_ref, wv_ref, out_ref,
    wq, wk, wv, acc, send, send_scale, recv, recv_scale,
    dq_ref, dkv_ref, total, own, near, part, part_scale, far, far_scale,
    w_sem, send_sem, recv_sem, send_scale_sem, recv_scale_sem,
    dq_sem, own_sem, near_send_sem, near_sem, part_sem, far_sem, part_scale_sem, far_scale_sem,
):
    me = lax.axis_index("tp")
    chips = n_ctx // 2
    place = lax.axis_index("ctx")
    chip, core = place // 2, lax.rem(place, 2)
    sibling = 2 * chip + 1 - core
    tokens, kv_width = dkv_ref.shape
    kv_half = kv_width // 2
    group = tokens // 8
    chunk_rows = out_ref.shape[0]
    sub_rows = acc.shape[0]
    subs = chunk_rows // sub_rows
    steps = 2 * (n - 1) * subs

    def plan(i):
        way = lax.rem(i, 2)
        rightward = jnp.where(me < n // 2, 1 - way, way)
        sub = lax.rem(i // 2, subs)
        step = i // (2 * subs)
        chunk = jnp.where(rightward == 1, n - 1 - step, step)
        active = jnp.where(rightward == 1, chunk > me, chunk < me)
        return rightward, chunk, sub, active

    def weight_copies(chunk, sub):
        at = chunk * subs + sub
        rows = pl.ds(pl.multiple_of(at * sub_rows, sub_rows), sub_rows)
        return [
            pltpu.make_async_copy(src.at[rows, :], dst.at[rows, :], w_sem.at[j, at])
            for j, (src, dst) in enumerate(((wq_ref, wq), (wk_ref, wk), (wv_ref, wv)))
        ]

    def remote(rightward, chunk, sub):
        slot = chunk * subs + sub
        to = jnp.where(rightward == 1, jnp.minimum(me + 1, n - 1), jnp.maximum(me - 1, 0))
        return [
            pltpu.make_async_remote_copy(
                src_ref=s.at[slot],
                dst_ref=r.at[rightward, slot],
                send_sem=ss.at[slot],
                recv_sem=rs.at[rightward, slot],
                device_id={"tp": to},
                device_id_type=MESH,
            )
            for s, r, ss, rs in (
                (send, recv, send_sem, recv_sem),
                (send_scale, recv_scale, send_scale_sem, recv_scale_sem),
            )
        ]

    def own_term(chunk, sub):
        for copy in weight_copies(chunk, sub):
            copy.wait()
        at = chunk * subs + sub
        rows = pl.ds(pl.multiple_of(at * sub_rows, sub_rows), sub_rows)
        half = wk.shape[1]
        contract = ((1,), (1,))
        total = dot(wq[rows, :], dq_ref[...], contract)
        total = total + dot(wk[rows, :], dkv_ref[:, :half], contract)
        acc[...] = total + dot(wv[rows, :], dkv_ref[:, half:], contract)

    def add_received(rightward, chunk, sub):
        for copy in remote(rightward, chunk, sub):
            copy.wait_recv()
        slot = chunk * subs + sub
        scale = recv_scale[rightward, slot, 0:1, :]
        acc[...] += recv[rightward, slot].astype(jnp.int32).astype(jnp.float32) * scale

    @pl.loop(0, steps)
    def _(i):
        _, chunk, sub, active = plan(i)

        @pl.when(active)
        def _():
            for copy in weight_copies(chunk, sub):
                copy.start()

    @pl.loop(0, subs)
    def _(sub):
        for copy in weight_copies(me, sub):
            copy.start()

    barrier = pltpu.get_barrier_semaphore()

    @pl.when(me > 0)
    def _():
        pl.semaphore_signal(barrier, inc=1, device_id={"tp": jnp.maximum(me - 1, 0)}, device_id_type=MESH)

    @pl.when(me < n - 1)
    def _():
        pl.semaphore_signal(barrier, inc=1, device_id={"tp": jnp.minimum(me + 1, n - 1)}, device_id_type=MESH)

    for away in range(1, chips):
        other = 2 * lax.rem(chip + away, chips) + core
        pl.semaphore_signal(barrier, inc=1, device_id={"ctx": other}, device_id_type=MESH)
    pl.semaphore_signal(barrier, inc=1, device_id={"ctx": sibling}, device_id_type=MESH)
    peers = jnp.where(me > 0, 1, 0) + jnp.where(me < n - 1, 1, 0) + chips
    pl.semaphore_wait(barrier, peers)

    def token_rows(block):
        return pl.ds(pl.multiple_of(block * tokens, tokens), tokens)

    def load_own(j):
        return pltpu.make_async_copy(terms_ref.at[token_rows(2 * j + core), :], own.at[j], own_sem.at[j])

    def to_sibling(j):
        return pltpu.make_async_remote_copy(
            src_ref=terms_ref.at[token_rows(2 * j + 1 - core), :],
            dst_ref=near.at[j],
            send_sem=near_send_sem.at[j],
            recv_sem=near_sem.at[j],
            device_id={"ctx": sibling},
            device_id_type=MESH,
        )

    def to_owner(source, j):
        return [
            pltpu.make_async_remote_copy(
                src_ref=p.at[j],
                dst_ref=f.at[source],
                send_sem=ps.at[j],
                recv_sem=fs.at[source],
                device_id={"ctx": 2 * j + core},
                device_id_type=MESH,
            )
            for p, f, ps, fs in (
                (part, far, part_sem, far_sem),
                (part_scale, far_scale, part_scale_sem, far_scale_sem),
            )
        ]

    @pl.loop(0, chip + 1)
    def _(j):
        to_sibling(j).start()
        load_own(j).start()

    pltpu.make_async_copy(dq_hbm, dq_ref, dq_sem.at[0]).start()

    @pl.loop(0, chip)
    def _(j):
        load_own(j).wait()
        to_sibling(j).wait_recv()
        for r in range(8):
            rows = slice(r * group, (r + 1) * group)
            x = own[j, rows, :] + near[j, rows, :]
            largest = jnp.maximum(jnp.max(jnp.abs(x), axis=0, keepdims=True), 1e-30)
            part_scale[j, r : r + 1, :] = largest * (1.0 / 32767.0)
            part[j, rows, :] = jnp.round(x * (32767.0 / largest)).astype(jnp.int32).astype(jnp.int16)
        for copy in to_owner(chip, j):
            copy.start()

    load_own(chip).wait()
    to_sibling(chip).wait_recv()
    total[...] = own[chip] + near[chip]

    @pl.loop(chip + 1, chips)
    def _(j):
        for copy in to_owner(j, chip):
            copy.wait_recv()
        for r in range(8):
            rows = slice(r * group, (r + 1) * group)
            x = far[j, rows, :].astype(jnp.int32).astype(jnp.float32)
            total[rows, :] += x * far_scale[j, r : r + 1, :]

    for c in range(kv_half // HEAD_SIZE):
        cols = slice(c * HEAD_SIZE, (c + 1) * HEAD_SIZE)
        x = total[:, cols] * SCALE
        x = x * cos_ref[...] - pltpu.roll(x, HEAD_SIZE // 2, 1) * sin_ref[...]
        dkv_ref[:, cols] = x.astype(jnp.bfloat16)
    dkv_ref[:, kv_half:] = total[:, kv_half:].astype(jnp.bfloat16)

    pltpu.make_async_copy(dq_hbm, dq_ref, dq_sem.at[0]).wait()

    @pl.loop(0, chip + 1)
    def _(j):
        to_sibling(j).wait_send()

    @pl.loop(0, chip)
    def _(j):
        for copy in to_owner(chip, j):
            copy.wait_send()

    @pl.loop(0, steps)
    def _(i):
        rightward, chunk, sub, active = plan(i)

        @pl.when(active)
        def _():
            own_term(chunk, sub)

            @pl.when(jnp.where(rightward == 1, me > 0, me < n - 1))
            def _():
                add_received(rightward, chunk, sub)

            slot = chunk * subs + sub
            largest = jnp.maximum(jnp.max(jnp.abs(acc[...]), axis=0, keepdims=True), 1e-30)
            send_scale[slot] = jnp.broadcast_to(largest * (1.0 / 32767.0), send_scale.shape[1:])
            coded = jnp.round(acc[...] * (32767.0 / largest))
            send[slot] = coded.astype(jnp.int32).astype(jnp.int16)
            for copy in remote(rightward, chunk, sub):
                copy.start()

    @pl.loop(0, subs)
    def _(sub):
        own_term(me, sub)

        @pl.when(me > 0)
        def _():
            add_received(1, me, sub)

        @pl.when(me < n - 1)
        def _():
            add_received(0, me, sub)

        rows = pl.ds(pl.multiple_of(sub * sub_rows, sub_rows), sub_rows)
        out_ref[rows, :] = acc[...].astype(jnp.bfloat16)

    @pl.loop(0, steps)
    def _(i):
        rightward, chunk, sub, active = plan(i)

        @pl.when(active)
        def _():
            for copy in remote(rightward, chunk, sub):
                copy.wait_send()


def project(n_ctx, n, dq, terms, cosine, sine, w_query, key_weight, value_weight):
    tokens = dq.shape[0]
    kv_width = terms.shape[1]
    chips = n_ctx // 2
    width = w_query.shape[0]
    chunk_rows = width // n
    sub_rows = 320 if chunk_rows % 320 == 0 else chunk_rows
    slots = width // sub_rows
    vm = pl.BlockSpec(memory_space=pltpu.VMEM)
    hbm = pl.BlockSpec(memory_space=pl.ANY)
    dma = pltpu.SemaphoreType.DMA
    return pl.pallas_call(
        functools.partial(project_kernel, n_ctx, n),
        out_shape=jax.ShapeDtypeStruct((chunk_rows, tokens), jnp.bfloat16),
        in_specs=[hbm, hbm, vm, vm, hbm, hbm, hbm],
        out_specs=vm,
        scratch_shapes=[
            pltpu.VMEM(w_query.shape, jnp.bfloat16),
            pltpu.VMEM(key_weight.shape, jnp.bfloat16),
            pltpu.VMEM(value_weight.shape, jnp.bfloat16),
            pltpu.VMEM((sub_rows, tokens), jnp.float32),
            pltpu.VMEM((slots, sub_rows, tokens), jnp.int16),
            pltpu.VMEM((slots, 8, tokens), jnp.float32),
            pltpu.VMEM((2, slots, sub_rows, tokens), jnp.int16),
            pltpu.VMEM((2, slots, 8, tokens), jnp.float32),
            pltpu.VMEM(dq.shape, jnp.bfloat16),
            pltpu.VMEM((tokens, kv_width), jnp.bfloat16),
            pltpu.VMEM((tokens, kv_width), jnp.float32),
            pltpu.VMEM((chips, tokens, kv_width), jnp.float32),
            pltpu.VMEM((chips, tokens, kv_width), jnp.float32),
            pltpu.VMEM((chips, tokens, kv_width), jnp.int16),
            pltpu.VMEM((chips, 8, kv_width), jnp.float32),
            pltpu.VMEM((chips, tokens, kv_width), jnp.int16),
            pltpu.VMEM((chips, 8, kv_width), jnp.float32),
            dma((3, slots)),
            dma((slots,)),
            dma((2, slots)),
            dma((slots,)),
            dma((2, slots)),
        ]
        + [dma((1,))]
        + [dma((chips,))] * 7,
        compiler_params=pltpu.CompilerParams(
            collective_id=2, has_side_effects=True, vmem_limit_bytes=VMEM_BYTES
        ),
        name="project",
    )(dq, terms, cosine, sine, w_query, key_weight, value_weight)


def local(
    n_ctx,
    n_tp,
    query,
    key_projected,
    value,
    attention_output,
    output_gradient,
    lse,
    block_mask,
    positions,
    segments,
    w_query,
    key_weight,
    value_weight,
):
    tok_rows = query.shape[0]
    q_start = lax.axis_index("ctx") * tok_rows
    cosine, sine = rope_tables(positions, HEAD_SIZE)
    kv_blocks, *prepared = gather(
        n_ctx, key_projected, value, query, output_gradient, attention_output, cosine, sine
    )
    kv_whole = kv_blocks.reshape(n_ctx * tok_rows, kv_blocks.shape[-1])
    seg_row = lax.dynamic_slice_in_dim(segments, q_start, tok_rows).reshape(1, tok_rows)
    first_tile = (q_start // TILE).astype(jnp.int32).reshape(1)
    query_grad, terms = attention(
        first_tile, block_mask, prepared, lse, cosine, sine, kv_whole, seg_row
    )
    return project(n_ctx, n_tp, query_grad, terms, cosine, sine, w_query, key_weight, value_weight)


def solution(mesh):
    in_specs = (
        P("ctx", "tp"),
        P("ctx", "tp"),
        P("ctx", "tp"),
        P("ctx", "tp"),
        P("ctx", "tp"),
        P("tp", "ctx"),
        P(),
        P("ctx"),
        P(),
        P(None, "tp"),
        P(None, "tp"),
        P(None, "tp"),
    )
    out_specs = P("tp", "ctx")
    body = functools.partial(local, mesh.shape["ctx"], mesh.shape["tp"])
    return jax.shard_map(body, mesh=mesh, in_specs=in_specs, out_specs=out_specs, check_vma=False)
```

```python
import functools

import jax
import jax.numpy as jnp
from jax import lax
from jax.experimental import pallas as pl
from jax.experimental.pallas import tpu as pltpu
from jax.sharding import PartitionSpec as P

QUERY_HEADS = 40
KEY_VALUE_HEADS = 8
HEAD_SIZE = 128
TILE = 128
GROUP = QUERY_HEADS // KEY_VALUE_HEADS
SCALE = HEAD_SIZE ** (-0.5)
MESH = pl.DeviceIdType.MESH
PROJECT_BYTES = 60 * 1024 * 1024
ATTENTION_BYTES = 56 * 1024 * 1024

rope_base = 1000000.0


def rope_tables(positions, head_dim):
    half = head_dim // 2
    exponent = jnp.arange(half).astype(jnp.float32) * (2.0 / head_dim)
    inverse = jnp.power(jnp.float32(rope_base), -exponent)
    angles = positions.astype(jnp.float32)[:, None] * inverse[None, :]
    cosine_table = jnp.cos(angles)
    sine_table = jnp.sin(angles)
    return (
        jnp.concatenate([cosine_table, cosine_table], 1),
        jnp.concatenate([-sine_table, sine_table], 1),
    )


def dot(a, b, dims=((1,), (0,))):
    return lax.dot_general(a, b, (dims, ((), ())), preferred_element_type=jnp.float32)


def gather_kernel(
    n, kp_hbm, v_hbm, q_hbm, do_hbm, ao_hbm, cos_ref, sin_ref,
    kv_ref, qs_ref, dos_ref, qt_ref, dot_ref, delta_ref,
    kp_ref, q_ref, do_ref, ao_ref, load_sem, send_sem, recv_sem, pass_sem, pass_recv_sem,
):
    me = lax.axis_index("ctx")
    chip, core = me // 2, lax.rem(me, 2)
    sibling = 2 * chip + 1 - core
    chips = n // 2
    tokens, kv_cols = kp_ref.shape
    heads = q_ref.shape[1] // HEAD_SIZE
    q_tiles = tokens // TILE
    loads = [
        pltpu.make_async_copy(src, dst, load_sem.at[j])
        for j, (src, dst) in enumerate(
            (
                (kp_hbm, kp_ref),
                (v_hbm, kv_ref.at[me, :, pl.ds(kv_cols, kv_cols)]),
                (q_hbm, q_ref),
                (do_hbm, do_ref),
                (ao_hbm, ao_ref),
            )
        )
    ]
    for copy in loads:
        copy.start()

    barrier = pltpu.get_barrier_semaphore()
    for away in range(1, chips):
        other = 2 * lax.rem(chip + away, chips) + core
        pl.semaphore_signal(barrier, inc=1, device_id={"ctx": other}, device_id_type=MESH)
    pl.semaphore_signal(barrier, inc=1, device_id={"ctx": sibling}, device_id_type=MESH)

    loads[0].wait()
    for c in range(kv_cols // HEAD_SIZE):
        cols = slice(c * HEAD_SIZE, (c + 1) * HEAD_SIZE)
        x = kp_ref[:, cols].astype(jnp.float32)
        x = x * cos_ref[...] + pltpu.roll(x, HEAD_SIZE // 2, 1) * sin_ref[...]
        kv_ref[me, :, cols] = x.astype(jnp.bfloat16)
    loads[1].wait()

    def direct(source, target):
        slot = 2 * source + core
        return pltpu.make_async_remote_copy(
            src_ref=kv_ref.at[slot],
            dst_ref=kv_ref.at[slot],
            send_sem=send_sem.at[target],
            recv_sem=recv_sem.at[source],
            device_id={"ctx": 2 * target + core},
            device_id_type=MESH,
        )

    def handed(source, from_core):
        slot = 2 * source + from_core
        return pltpu.make_async_remote_copy(
            src_ref=kv_ref.at[slot],
            dst_ref=kv_ref.at[slot],
            send_sem=pass_sem.at[source],
            recv_sem=pass_recv_sem.at[source],
            device_id={"ctx": sibling},
            device_id_type=MESH,
        )

    pl.semaphore_wait(barrier, chips)
    for away in range(chips - 1, 0, -1):

        @pl.when(chip + away < chips)
        def _():
            direct(chip, jnp.minimum(chip + away, chips - 1)).start()

    handed(chip, core).start()
    for copy in loads[2:]:
        copy.wait()

    @pl.loop(0, q_tiles * heads)
    def _(i):
        t, h = i // heads, lax.rem(i, heads)
        c, g = h // GROUP, lax.rem(h, GROUP)
        rows = pl.ds(pl.multiple_of(t * TILE, TILE), TILE)
        cols = pl.ds(pl.multiple_of(h * HEAD_SIZE, HEAD_SIZE), HEAD_SIZE)
        part = pl.ds(pl.multiple_of(g * TILE, TILE), TILE)
        x = q_ref[rows, cols].astype(jnp.float32)
        x = x * cos_ref[rows, :] + pltpu.roll(x, HEAD_SIZE // 2, 1) * sin_ref[rows, :]
        xb = x.astype(jnp.bfloat16)
        qs_ref[t, c, part, :] = xb
        qt_ref[t, c, :, part] = xb.astype(jnp.float32).T.astype(jnp.bfloat16)
        y = do_ref[rows, cols]
        dos_ref[t, c, part, :] = y
        y_turned = y.astype(jnp.float32).T
        dot_ref[t, c, :, part] = y_turned.astype(jnp.bfloat16)
        o_turned = ao_ref[rows, cols].astype(jnp.float32).T
        delta_ref[t, c, :, part] = jnp.sum(y_turned * o_turned, axis=0, keepdims=True)

    for away in range(1, chips):

        @pl.when(chip - away >= 0)
        def _():
            source = jnp.maximum(chip - away, 0)
            direct(source, chip).wait_recv()
            handed(source, core).start()

    for away in range(chips):

        @pl.when(chip - away >= 0)
        def _():
            source = jnp.maximum(chip - away, 0)
            handed(source, 1 - core).wait_recv()
            handed(source, core).wait_send()

    for away in range(1, chips):

        @pl.when(chip + away < chips)
        def _():
            direct(chip, jnp.minimum(chip + away, chips - 1)).wait_send()


def gather(n, key_projected, value, query, grad, attention_output, cosine, sine):
    tokens, kv_cols = key_projected.shape
    kv_local = kv_cols // HEAD_SIZE
    q_tiles = tokens // TILE
    wide = GROUP * TILE
    vm = pl.BlockSpec(memory_space=pltpu.VMEM)
    hbm = pl.BlockSpec(memory_space=pltpu.HBM)
    dma = pltpu.SemaphoreType.DMA
    stacked = jax.ShapeDtypeStruct((q_tiles, kv_local, wide, HEAD_SIZE), jnp.bfloat16)
    turned = jax.ShapeDtypeStruct((q_tiles, kv_local, HEAD_SIZE, wide), jnp.bfloat16)
    return pl.pallas_call(
        functools.partial(gather_kernel, n),
        out_shape=(
            jax.ShapeDtypeStruct((n, tokens, 2 * kv_cols), jnp.bfloat16),
            stacked,
            stacked,
            turned,
            turned,
            jax.ShapeDtypeStruct((q_tiles, kv_local, 1, wide), jnp.float32),
        ),
        in_specs=[hbm] * 5 + [vm, vm],
        out_specs=(vm,) * 6,
        scratch_shapes=[pltpu.VMEM(key_projected.shape, jnp.bfloat16)]
        + [pltpu.VMEM(query.shape, jnp.bfloat16)] * 3
        + [dma((5,))]
        + [dma((n // 2,))] * 4,
        compiler_params=pltpu.CompilerParams(
            collective_id=1, has_side_effects=True, vmem_limit_bytes=ATTENTION_BYTES
        ),
        name="gather",
    )(key_projected, value, query, grad, attention_output, cosine, sine)


def attention_kernel(
    start_ref, mask_ref, qs, dos, qt_s, dot_s, lse_ref, delta_s, cos_ref, sin_ref, kv_ref, segq_ref, segk_ref,
    dq_ref, dkv_ref, lse_s, dqt, needed_ref,
):
    tokens = dq_ref.shape[0]
    kv_local = kv_ref.shape[1] // (2 * HEAD_SIZE)
    q_tiles = tokens // TILE
    first_tile = start_ref[0]
    dkv_ref[...] = jnp.zeros_like(dkv_ref)
    dqt[...] = jnp.zeros_like(dqt)
    for t in range(q_tiles):
        for h in range(kv_local * GROUP):
            c, g = h // GROUP, h % GROUP
            lse_s[t, c, :, g * TILE : (g + 1) * TILE] = lse_ref[h : h + 1, t * TILE : (t + 1) * TILE]

    def terms(t, k_tiles, allowed):
        spans = [pl.ds(pl.multiple_of(k * TILE, TILE), TILE) for k in k_tiles]
        for c in range(kv_local):
            key_cols = slice(c * HEAD_SIZE, (c + 1) * HEAD_SIZE)
            val_cols = slice((kv_local + c) * HEAD_SIZE, (kv_local + c + 1) * HEAD_SIZE)
            k = jnp.concatenate([kv_ref[span, key_cols] for span in spans], 0)
            v = jnp.concatenate([kv_ref[span, val_cols] for span in spans], 0)
            scores = dot(k, qt_s[t, c]) * SCALE
            probs = jnp.exp(scores - lse_s[t, c])
            if allowed is not None:
                probs = jnp.where(allowed, probs, 0.0)
            dscore = probs * (dot(v, dot_s[t, c]) - delta_s[t, c])
            pb = probs.astype(jnp.bfloat16)
            db = dscore.astype(jnp.bfloat16)
            dk = dot(db, qs[t, c])
            dv = dot(pb, dos[t, c])
            for j, span in enumerate(spans):
                dkv_ref[span, key_cols] += dk[j * TILE : (j + 1) * TILE]
                dkv_ref[span, val_cols] += dv[j * TILE : (j + 1) * TILE]
            kt = k.astype(jnp.float32).T.astype(jnp.bfloat16)
            dqt[t, c] += dot(kt, db)

    for t in range(q_tiles):
        own = first_tile + t

        def note(k_tile, count):
            needed_ref[count] = k_tile
            return count + jnp.where(mask_ref[own, k_tile] > 0, 1, 0)

        count = lax.fori_loop(0, own, note, jnp.int32(0))

        @pl.loop(0, count // 2)
        def _(i):
            terms(t, (needed_ref[2 * i], needed_ref[2 * i + 1]), None)

        row = lax.broadcasted_iota(jnp.int32, (TILE, TILE), 0)
        col = lax.broadcasted_iota(jnp.int32, (TILE, TILE), 1)
        seg_k = segk_ref[t * TILE : (t + 1) * TILE, :]
        seg_q = segq_ref[:, t * TILE : (t + 1) * TILE]
        inner = jnp.where((row <= col) & (seg_k == seg_q), 1.0, 0.0)
        inner = jnp.concatenate([inner] * GROUP, 1)

        @pl.when(lax.rem(count, 2) == 1)
        def _():
            whole = jnp.concatenate([jnp.ones_like(inner), inner], 0)
            terms(t, (needed_ref[count - 1], own), whole > 0.5)

        @pl.when(lax.rem(count, 2) == 0)
        def _():
            terms(t, (own,), inner > 0.5)

        rows = slice(t * TILE, (t + 1) * TILE)
        cosine = cos_ref[rows, :]
        sine = sin_ref[rows, :]
        for h in range(kv_local * GROUP):
            c, g = h // GROUP, h % GROUP
            x = (dqt[t, c, :, g * TILE : (g + 1) * TILE] * SCALE).T
            x = x * cosine - pltpu.roll(x, HEAD_SIZE // 2, 1) * sine
            dq_ref[rows, h * HEAD_SIZE : (h + 1) * HEAD_SIZE] = x.astype(jnp.bfloat16)


def attention(first_tile, block_mask, prepared, lse, cosine, sine, kv_whole, seg_row):
    qs, dos, turned_q, turned_do, delta = prepared
    q_tiles, kv_local, wide, _ = qs.shape
    tokens = q_tiles * TILE
    vm = pl.BlockSpec(memory_space=pltpu.VMEM)
    sm = pl.BlockSpec(memory_space=pltpu.SMEM)
    return pl.pallas_call(
        attention_kernel,
        out_shape=(
            jax.ShapeDtypeStruct((tokens, kv_local * GROUP * HEAD_SIZE), jnp.bfloat16),
            jax.ShapeDtypeStruct(kv_whole.shape, jnp.float32),
        ),
        in_specs=[sm, sm] + [vm] * 11,
        out_specs=(vm, vm),
        scratch_shapes=[
            pltpu.VMEM((q_tiles, kv_local, 1, wide), jnp.float32),
            pltpu.VMEM((q_tiles, kv_local, HEAD_SIZE, wide), jnp.float32),
            pltpu.SMEM((block_mask.shape[0],), jnp.int32),
        ],
        compiler_params=pltpu.CompilerParams(vmem_limit_bytes=ATTENTION_BYTES),
        name="attention",
    )(
        first_tile, block_mask, qs, dos, turned_q, turned_do, lse, delta, cosine, sine, kv_whole,
        seg_row, seg_row.reshape(tokens, 1),
    )


def project_kernel(
    n_ctx, n, dq_hbm, terms_ref, cos_ref, sin_ref, wq_ref, wk_ref, wv_ref, out_ref,
    wq, wk, wv, acc, send, send_scale, recv, recv_scale,
    dq_ref, dkv_ref, total, own, near, part, part_scale, far, far_scale,
    w_sem, send_sem, recv_sem, send_scale_sem, recv_scale_sem,
    dq_sem, own_sem, near_send_sem, near_sem, part_sem, far_sem, part_scale_sem, far_scale_sem,
):
    me = lax.axis_index("tp")
    chips = n_ctx // 2
    place = lax.axis_index("ctx")
    chip, core = place // 2, lax.rem(place, 2)
    sibling = 2 * chip + 1 - core
    tokens, kv_width = dkv_ref.shape
    kv_half = kv_width // 2
    group = tokens // 8
    chunk_rows = out_ref.shape[0]
    sub_rows = acc.shape[0]
    subs = chunk_rows // sub_rows
    steps = 2 * (n - 1) * subs

    def plan(i):
        way = lax.rem(i, 2)
        rightward = jnp.where(me < n // 2, 1 - way, way)
        sub = lax.rem(i // 2, subs)
        step = i // (2 * subs)
        chunk = jnp.where(rightward == 1, n - 1 - step, step)
        active = jnp.where(rightward == 1, chunk > me, chunk < me)
        return rightward, chunk, sub, active

    def weight_copies(chunk, sub):
        at = chunk * subs + sub
        rows = pl.ds(pl.multiple_of(at * sub_rows, sub_rows), sub_rows)
        return [
            pltpu.make_async_copy(src.at[rows, :], dst.at[rows, :], w_sem.at[j, at])
            for j, (src, dst) in enumerate(((wq_ref, wq), (wk_ref, wk), (wv_ref, wv)))
        ]

    def remote(rightward, chunk, sub):
        slot = chunk * subs + sub
        to = jnp.where(rightward == 1, jnp.minimum(me + 1, n - 1), jnp.maximum(me - 1, 0))
        return [
            pltpu.make_async_remote_copy(
                src_ref=s.at[slot],
                dst_ref=r.at[rightward, slot],
                send_sem=ss.at[slot],
                recv_sem=rs.at[rightward, slot],
                device_id={"tp": to},
                device_id_type=MESH,
            )
            for s, r, ss, rs in (
                (send, recv, send_sem, recv_sem),
                (send_scale, recv_scale, send_scale_sem, recv_scale_sem),
            )
        ]

    def own_term(chunk, sub):
        for copy in weight_copies(chunk, sub):
            copy.wait()
        at = chunk * subs + sub
        rows = pl.ds(pl.multiple_of(at * sub_rows, sub_rows), sub_rows)
        half = wk.shape[1]
        contract = ((1,), (1,))
        total = dot(wq[rows, :], dq_ref[...], contract)
        total = total + dot(wk[rows, :], dkv_ref[:, :half], contract)
        acc[...] = total + dot(wv[rows, :], dkv_ref[:, half:], contract)

    def add_received(rightward, chunk, sub):
        for copy in remote(rightward, chunk, sub):
            copy.wait_recv()
        slot = chunk * subs + sub
        scale = recv_scale[rightward, slot, 0:1, :]
        acc[...] += recv[rightward, slot].astype(jnp.int32).astype(jnp.float32) * scale

    @pl.loop(0, steps)
    def _(i):
        _, chunk, sub, active = plan(i)

        @pl.when(active)
        def _():
            for copy in weight_copies(chunk, sub):
                copy.start()

    @pl.loop(0, subs)
    def _(sub):
        for copy in weight_copies(me, sub):
            copy.start()

    barrier = pltpu.get_barrier_semaphore()

    @pl.when(me > 0)
    def _():
        pl.semaphore_signal(barrier, inc=1, device_id={"tp": jnp.maximum(me - 1, 0)}, device_id_type=MESH)

    @pl.when(me < n - 1)
    def _():
        pl.semaphore_signal(barrier, inc=1, device_id={"tp": jnp.minimum(me + 1, n - 1)}, device_id_type=MESH)

    for away in range(1, chips):
        other = 2 * lax.rem(chip + away, chips) + core
        pl.semaphore_signal(barrier, inc=1, device_id={"ctx": other}, device_id_type=MESH)
    pl.semaphore_signal(barrier, inc=1, device_id={"ctx": sibling}, device_id_type=MESH)
    peers = jnp.where(me > 0, 1, 0) + jnp.where(me < n - 1, 1, 0) + chips
    pl.semaphore_wait(barrier, peers)

    def token_rows(block):
        return pl.ds(pl.multiple_of(block * tokens, tokens), tokens)

    def load_own(j):
        return pltpu.make_async_copy(terms_ref.at[token_rows(2 * j + core), :], own.at[j], own_sem.at[j])

    def to_sibling(j):
        return pltpu.make_async_remote_copy(
            src_ref=terms_ref.at[token_rows(2 * j + 1 - core), :],
            dst_ref=near.at[j],
            send_sem=near_send_sem.at[j],
            recv_sem=near_sem.at[j],
            device_id={"ctx": sibling},
            device_id_type=MESH,
        )

    def to_owner(source, j):
        return [
            pltpu.make_async_remote_copy(
                src_ref=p.at[j],
                dst_ref=f.at[source],
                send_sem=ps.at[j],
                recv_sem=fs.at[source],
                device_id={"ctx": 2 * j + core},
                device_id_type=MESH,
            )
            for p, f, ps, fs in (
                (part, far, part_sem, far_sem),
                (part_scale, far_scale, part_scale_sem, far_scale_sem),
            )
        ]

    @pl.loop(0, chip + 1)
    def _(j):
        to_sibling(j).start()
        load_own(j).start()

    pltpu.make_async_copy(dq_hbm, dq_ref, dq_sem.at[0]).start()

    @pl.loop(0, chip)
    def _(j):
        load_own(j).wait()
        to_sibling(j).wait_recv()
        for r in range(8):
            rows = slice(r * group, (r + 1) * group)
            x = own[j, rows, :] + near[j, rows, :]
            largest = jnp.maximum(jnp.max(jnp.abs(x), axis=0, keepdims=True), 1e-30)
            part_scale[j, r : r + 1, :] = largest * (1.0 / 32767.0)
            part[j, rows, :] = jnp.round(x * (32767.0 / largest)).astype(jnp.int32).astype(jnp.int16)
        for copy in to_owner(chip, j):
            copy.start()

    load_own(chip).wait()
    to_sibling(chip).wait_recv()
    total[...] = own[chip] + near[chip]

    @pl.loop(chip + 1, chips)
    def _(j):
        for copy in to_owner(j, chip):
            copy.wait_recv()
        for r in range(8):
            rows = slice(r * group, (r + 1) * group)
            x = far[j, rows, :].astype(jnp.int32).astype(jnp.float32)
            total[rows, :] += x * far_scale[j, r : r + 1, :]

    for c in range(kv_half // HEAD_SIZE):
        cols = slice(c * HEAD_SIZE, (c + 1) * HEAD_SIZE)
        x = total[:, cols] * SCALE
        x = x * cos_ref[...] - pltpu.roll(x, HEAD_SIZE // 2, 1) * sin_ref[...]
        dkv_ref[:, cols] = x.astype(jnp.bfloat16)
    dkv_ref[:, kv_half:] = total[:, kv_half:].astype(jnp.bfloat16)

    pltpu.make_async_copy(dq_hbm, dq_ref, dq_sem.at[0]).wait()

    @pl.loop(0, chip + 1)
    def _(j):
        to_sibling(j).wait_send()

    @pl.loop(0, chip)
    def _(j):
        for copy in to_owner(chip, j):
            copy.wait_send()

    @pl.loop(0, steps)
    def _(i):
        rightward, chunk, sub, active = plan(i)

        @pl.when(active)
        def _():
            own_term(chunk, sub)

            @pl.when(jnp.where(rightward == 1, me > 0, me < n - 1))
            def _():
                add_received(rightward, chunk, sub)

            slot = chunk * subs + sub
            largest = jnp.maximum(jnp.max(jnp.abs(acc[...]), axis=0, keepdims=True), 1e-30)
            send_scale[slot] = jnp.broadcast_to(largest * (1.0 / 32767.0), send_scale.shape[1:])
            coded = jnp.round(acc[...] * (32767.0 / largest))
            send[slot] = coded.astype(jnp.int32).astype(jnp.int16)
            for copy in remote(rightward, chunk, sub):
                copy.start()

    @pl.loop(0, subs)
    def _(sub):
        own_term(me, sub)

        @pl.when(me > 0)
        def _():
            add_received(1, me, sub)

        @pl.when(me < n - 1)
        def _():
            add_received(0, me, sub)

        rows = pl.ds(pl.multiple_of(sub * sub_rows, sub_rows), sub_rows)
        out_ref[rows, :] = acc[...].astype(jnp.bfloat16)

    @pl.loop(0, steps)
    def _(i):
        rightward, chunk, sub, active = plan(i)

        @pl.when(active)
        def _():
            for copy in remote(rightward, chunk, sub):
                copy.wait_send()


def project(n_ctx, n, dq, terms, cosine, sine, w_query, key_weight, value_weight):
    tokens = dq.shape[0]
    kv_width = terms.shape[1]
    chips = n_ctx // 2
    width = w_query.shape[0]
    chunk_rows = width // n
    sub_rows = 320 if chunk_rows % 320 == 0 else chunk_rows
    slots = width // sub_rows
    vm = pl.BlockSpec(memory_space=pltpu.VMEM)
    hbm = pl.BlockSpec(memory_space=pl.ANY)
    dma = pltpu.SemaphoreType.DMA
    return pl.pallas_call(
        functools.partial(project_kernel, n_ctx, n),
        out_shape=jax.ShapeDtypeStruct((chunk_rows, tokens), jnp.bfloat16),
        in_specs=[hbm, hbm, vm, vm, hbm, hbm, hbm],
        out_specs=vm,
        scratch_shapes=[
            pltpu.VMEM(w_query.shape, jnp.bfloat16),
            pltpu.VMEM(key_weight.shape, jnp.bfloat16),
            pltpu.VMEM(value_weight.shape, jnp.bfloat16),
            pltpu.VMEM((sub_rows, tokens), jnp.float32),
            pltpu.VMEM((slots, sub_rows, tokens), jnp.int16),
            pltpu.VMEM((slots, 8, tokens), jnp.float32),
            pltpu.VMEM((2, slots, sub_rows, tokens), jnp.int16),
            pltpu.VMEM((2, slots, 8, tokens), jnp.float32),
            pltpu.VMEM(dq.shape, jnp.bfloat16),
            pltpu.VMEM((tokens, kv_width), jnp.bfloat16),
            pltpu.VMEM((tokens, kv_width), jnp.float32),
            pltpu.VMEM((chips, tokens, kv_width), jnp.float32),
            pltpu.VMEM((chips, tokens, kv_width), jnp.float32),
            pltpu.VMEM((chips, tokens, kv_width), jnp.int16),
            pltpu.VMEM((chips, 8, kv_width), jnp.float32),
            pltpu.VMEM((chips, tokens, kv_width), jnp.int16),
            pltpu.VMEM((chips, 8, kv_width), jnp.float32),
            dma((3, slots)),
            dma((slots,)),
            dma((2, slots)),
            dma((slots,)),
            dma((2, slots)),
        ]
        + [dma((1,))]
        + [dma((chips,))] * 7,
        compiler_params=pltpu.CompilerParams(
            collective_id=2, has_side_effects=True, vmem_limit_bytes=PROJECT_BYTES
        ),
        name="project",
    )(dq, terms, cosine, sine, w_query, key_weight, value_weight)


def local(
    n_ctx,
    n_tp,
    query,
    key_projected,
    value,
    attention_output,
    output_gradient,
    lse,
    block_mask,
    positions,
    segments,
    w_query,
    key_weight,
    value_weight,
):
    tok_rows = query.shape[0]
    q_start = lax.axis_index("ctx") * tok_rows
    cosine, sine = rope_tables(positions, HEAD_SIZE)
    kv_blocks, *prepared = gather(
        n_ctx, key_projected, value, query, output_gradient, attention_output, cosine, sine
    )
    kv_whole = kv_blocks.reshape(n_ctx * tok_rows, kv_blocks.shape[-1])
    seg_row = lax.dynamic_slice_in_dim(segments, q_start, tok_rows).reshape(1, tok_rows)
    first_tile = (q_start // TILE).astype(jnp.int32).reshape(1)
    query_grad, terms = attention(
        first_tile, block_mask, prepared, lse, cosine, sine, kv_whole, seg_row
    )
    return project(n_ctx, n_tp, query_grad, terms, cosine, sine, w_query, key_weight, value_weight)


def solution(mesh):
    in_specs = (
        P("ctx", "tp"),
        P("ctx", "tp"),
        P("ctx", "tp"),
        P("ctx", "tp"),
        P("ctx", "tp"),
        P("tp", "ctx"),
        P(),
        P("ctx"),
        P(),
        P(None, "tp"),
        P(None, "tp"),
        P(None, "tp"),
    )
    out_specs = P("tp", "ctx")
    body = functools.partial(local, mesh.shape["ctx"], mesh.shape["tp"])
    return jax.shard_map(body, mesh=mesh, in_specs=in_specs, out_specs=out_specs, check_vma=False)
```

```python
import functools

import jax
import jax.numpy as jnp
from jax import lax
from jax.experimental import pallas as pl
from jax.experimental.pallas import tpu as pltpu
from jax.sharding import PartitionSpec as P

QUERY_HEADS = 40
KEY_VALUE_HEADS = 8
HEAD_SIZE = 128
TILE = 128
GROUP = QUERY_HEADS // KEY_VALUE_HEADS
SCALE = HEAD_SIZE ** (-0.5)
MESH = pl.DeviceIdType.MESH
PROJECT_BYTES = 60 * 1024 * 1024
ATTENTION_BYTES = 56 * 1024 * 1024

rope_base = 1000000.0


def rope_tables(positions, head_dim):
    half = head_dim // 2
    exponent = jnp.arange(half).astype(jnp.float32) * (2.0 / head_dim)
    inverse = jnp.power(jnp.float32(rope_base), -exponent)
    angles = positions.astype(jnp.float32)[:, None] * inverse[None, :]
    cosine_table = jnp.cos(angles)
    sine_table = jnp.sin(angles)
    return (
        jnp.concatenate([cosine_table, cosine_table], 1),
        jnp.concatenate([-sine_table, sine_table], 1),
    )


def dot(a, b, dims=((1,), (0,))):
    return lax.dot_general(a, b, (dims, ((), ())), preferred_element_type=jnp.float32)


def line_ends(at, n):
    is_end = (at == 0) | (at == n - 1)
    is_next = (at == 1) | (at == n - 2)
    mate = jnp.where(at == 0, 1, jnp.where(at == n - 1, n - 2, jnp.where(at == 1, 0, n - 1)))
    return is_end, is_next, mate


def gather_kernel(
    n, n_tp, kp_hbm, v_hbm, q_hbm, do_hbm, ao_hbm, cos_ref, sin_ref, wk_hbm, wv_hbm,
    kv_ref, qs_ref, dos_ref, qt_ref, dot_ref, delta_ref, far_ref,
    kp_ref, q_ref, do_ref, ao_ref, load_sem, far_send_sem, far_recv_sem,
    send_sem, recv_sem, pass_sem, pass_recv_sem,
):
    me = lax.axis_index("ctx")
    chip, core = me // 2, lax.rem(me, 2)
    sibling = 2 * chip + 1 - core
    chips = n // 2
    tokens, kv_cols = kp_ref.shape
    heads = q_ref.shape[1] // HEAD_SIZE
    q_tiles = tokens // TILE
    loads = [
        pltpu.make_async_copy(src, dst, load_sem.at[j])
        for j, (src, dst) in enumerate(
            (
                (kp_hbm, kp_ref),
                (v_hbm, kv_ref.at[me, :, pl.ds(kv_cols, kv_cols)]),
                (q_hbm, q_ref),
                (do_hbm, do_ref),
                (ao_hbm, ao_ref),
            )
        )
    ]
    for copy in loads:
        copy.start()

    barrier = pltpu.get_barrier_semaphore()
    for away in range(1, chips):
        other = 2 * lax.rem(chip + away, chips) + core
        pl.semaphore_signal(barrier, inc=1, device_id={"ctx": other}, device_id_type=MESH)
    pl.semaphore_signal(barrier, inc=1, device_id={"ctx": sibling}, device_id_type=MESH)

    line = lax.axis_index("tp")
    is_end, is_next, mate = line_ends(line, n_tp)
    half = far_ref.shape[1] // 2
    chunk = jnp.where(line == 0, n_tp - 1, 0)

    def far_weights():
        rows = pl.ds(pl.multiple_of(chunk * 2 * half + core * half, half), half)
        there = pl.ds(pl.multiple_of(core * half, half), half)
        return [
            pltpu.make_async_remote_copy(
                src_ref=src.at[rows, :],
                dst_ref=far_ref.at[j, there, :],
                send_sem=far_send_sem.at[j],
                recv_sem=far_recv_sem.at[j],
                device_id={"tp": mate},
                device_id_type=MESH,
            )
            for j, src in enumerate((wk_hbm, wv_hbm))
        ]

    @pl.when(is_end | is_next)
    def _():
        pl.semaphore_signal(barrier, inc=1, device_id={"tp": mate}, device_id_type=MESH)

    loads[0].wait()
    for c in range(kv_cols // HEAD_SIZE):
        cols = slice(c * HEAD_SIZE, (c + 1) * HEAD_SIZE)
        x = kp_ref[:, cols].astype(jnp.float32)
        x = x * cos_ref[...] + pltpu.roll(x, HEAD_SIZE // 2, 1) * sin_ref[...]
        kv_ref[me, :, cols] = x.astype(jnp.bfloat16)
    loads[1].wait()

    def direct(source, target):
        slot = 2 * source + core
        return pltpu.make_async_remote_copy(
            src_ref=kv_ref.at[slot],
            dst_ref=kv_ref.at[slot],
            send_sem=send_sem.at[target],
            recv_sem=recv_sem.at[source],
            device_id={"ctx": 2 * target + core},
            device_id_type=MESH,
        )

    def handed(source, from_core):
        slot = 2 * source + from_core
        return pltpu.make_async_remote_copy(
            src_ref=kv_ref.at[slot],
            dst_ref=kv_ref.at[slot],
            send_sem=pass_sem.at[source],
            recv_sem=pass_recv_sem.at[source],
            device_id={"ctx": sibling},
            device_id_type=MESH,
        )

    pl.semaphore_wait(barrier, chips + jnp.where(is_end | is_next, 1, 0))
    for away in range(chips - 1, 0, -1):

        @pl.when(chip + away < chips)
        def _():
            direct(chip, jnp.minimum(chip + away, chips - 1)).start()

    handed(chip, core).start()

    @pl.when(is_end)
    def _():
        for copy in far_weights():
            copy.start()

    for copy in loads[2:]:
        copy.wait()

    @pl.loop(0, q_tiles * heads)
    def _(i):
        t, h = i // heads, lax.rem(i, heads)
        c, g = h // GROUP, lax.rem(h, GROUP)
        rows = pl.ds(pl.multiple_of(t * TILE, TILE), TILE)
        cols = pl.ds(pl.multiple_of(h * HEAD_SIZE, HEAD_SIZE), HEAD_SIZE)
        part = pl.ds(pl.multiple_of(g * TILE, TILE), TILE)
        x = q_ref[rows, cols].astype(jnp.float32)
        x = x * cos_ref[rows, :] + pltpu.roll(x, HEAD_SIZE // 2, 1) * sin_ref[rows, :]
        xb = x.astype(jnp.bfloat16)
        qs_ref[t, c, part, :] = xb
        qt_ref[t, c, :, part] = xb.astype(jnp.float32).T.astype(jnp.bfloat16)
        y = do_ref[rows, cols]
        dos_ref[t, c, part, :] = y
        y_turned = y.astype(jnp.float32).T
        dot_ref[t, c, :, part] = y_turned.astype(jnp.bfloat16)
        o_turned = ao_ref[rows, cols].astype(jnp.float32).T
        delta_ref[t, c, :, part] = jnp.sum(y_turned * o_turned, axis=0, keepdims=True)

    for away in range(1, chips):

        @pl.when(chip - away >= 0)
        def _():
            source = jnp.maximum(chip - away, 0)
            direct(source, chip).wait_recv()
            handed(source, core).start()

    for away in range(chips):

        @pl.when(chip - away >= 0)
        def _():
            source = jnp.maximum(chip - away, 0)
            handed(source, 1 - core).wait_recv()
            handed(source, core).wait_send()

    for away in range(1, chips):

        @pl.when(chip + away < chips)
        def _():
            direct(chip, jnp.minimum(chip + away, chips - 1)).wait_send()

    @pl.when(is_next)
    def _():
        for copy in far_weights():
            copy.wait_recv()

    @pl.when(is_end)
    def _():
        for copy in far_weights():
            copy.wait_send()


def gather(n, n_tp, key_projected, value, query, grad, attention_output, cosine, sine, key_weight, value_weight):
    tokens, kv_cols = key_projected.shape
    kv_local = kv_cols // HEAD_SIZE
    q_tiles = tokens // TILE
    wide = GROUP * TILE
    vm = pl.BlockSpec(memory_space=pltpu.VMEM)
    hbm = pl.BlockSpec(memory_space=pltpu.HBM)
    dma = pltpu.SemaphoreType.DMA
    stacked = jax.ShapeDtypeStruct((q_tiles, kv_local, wide, HEAD_SIZE), jnp.bfloat16)
    turned = jax.ShapeDtypeStruct((q_tiles, kv_local, HEAD_SIZE, wide), jnp.bfloat16)
    return pl.pallas_call(
        functools.partial(gather_kernel, n, n_tp),
        out_shape=(
            jax.ShapeDtypeStruct((n, tokens, 2 * kv_cols), jnp.bfloat16),
            stacked,
            stacked,
            turned,
            turned,
            jax.ShapeDtypeStruct((q_tiles, kv_local, 1, wide), jnp.float32),
            jax.ShapeDtypeStruct((2, key_weight.shape[0] // n_tp, kv_cols), jnp.bfloat16),
        ),
        in_specs=[hbm] * 5 + [vm, vm, hbm, hbm],
        out_specs=(vm,) * 6 + (pl.BlockSpec(memory_space=pl.ANY),),
        scratch_shapes=[pltpu.VMEM(key_projected.shape, jnp.bfloat16)]
        + [pltpu.VMEM(query.shape, jnp.bfloat16)] * 3
        + [dma((5,)), dma((2,)), dma((2,))]
        + [dma((n // 2,))] * 4,
        compiler_params=pltpu.CompilerParams(
            collective_id=1, has_side_effects=True, vmem_limit_bytes=ATTENTION_BYTES
        ),
        name="gather",
    )(key_projected, value, query, grad, attention_output, cosine, sine, key_weight, value_weight)


def attention_kernel(
    start_ref, mask_ref, qs, dos, qt_s, dot_s, lse_ref, delta_s, cos_ref, sin_ref, kv_ref, segq_ref, segk_ref,
    dq_ref, dkv_ref, lse_s, dqt, needed_ref,
):
    tokens = dq_ref.shape[0]
    kv_local = kv_ref.shape[1] // (2 * HEAD_SIZE)
    q_tiles = tokens // TILE
    first_tile = start_ref[0]
    dkv_ref[...] = jnp.zeros_like(dkv_ref)
    dqt[...] = jnp.zeros_like(dqt)
    for t in range(q_tiles):
        for h in range(kv_local * GROUP):
            c, g = h // GROUP, h % GROUP
            lse_s[t, c, :, g * TILE : (g + 1) * TILE] = lse_ref[h : h + 1, t * TILE : (t + 1) * TILE]

    def terms(t, k_tiles, allowed):
        spans = [pl.ds(pl.multiple_of(k * TILE, TILE), TILE) for k in k_tiles]
        for c in range(kv_local):
            key_cols = slice(c * HEAD_SIZE, (c + 1) * HEAD_SIZE)
            val_cols = slice((kv_local + c) * HEAD_SIZE, (kv_local + c + 1) * HEAD_SIZE)
            k = jnp.concatenate([kv_ref[span, key_cols] for span in spans], 0)
            v = jnp.concatenate([kv_ref[span, val_cols] for span in spans], 0)
            scores = dot(k, qt_s[t, c]) * SCALE
            probs = jnp.exp(scores - lse_s[t, c])
            if allowed is not None:
                probs = jnp.where(allowed, probs, 0.0)
            dscore = probs * (dot(v, dot_s[t, c]) - delta_s[t, c])
            pb = probs.astype(jnp.bfloat16)
            db = dscore.astype(jnp.bfloat16)
            dk = dot(db, qs[t, c])
            dv = dot(pb, dos[t, c])
            for j, span in enumerate(spans):
                dkv_ref[span, key_cols] += dk[j * TILE : (j + 1) * TILE]
                dkv_ref[span, val_cols] += dv[j * TILE : (j + 1) * TILE]
            kt = k.astype(jnp.float32).T.astype(jnp.bfloat16)
            dqt[t, c] += dot(kt, db)

    for t in range(q_tiles):
        own = first_tile + t

        def note(k_tile, count):
            needed_ref[count] = k_tile
            return count + jnp.where(mask_ref[own, k_tile] > 0, 1, 0)

        count = lax.fori_loop(0, own, note, jnp.int32(0))

        @pl.loop(0, count // 2)
        def _(i):
            terms(t, (needed_ref[2 * i], needed_ref[2 * i + 1]), None)

        row = lax.broadcasted_iota(jnp.int32, (TILE, TILE), 0)
        col = lax.broadcasted_iota(jnp.int32, (TILE, TILE), 1)
        seg_k = segk_ref[t * TILE : (t + 1) * TILE, :]
        seg_q = segq_ref[:, t * TILE : (t + 1) * TILE]
        inner = jnp.where((row <= col) & (seg_k == seg_q), 1.0, 0.0)
        inner = jnp.concatenate([inner] * GROUP, 1)

        @pl.when(lax.rem(count, 2) == 1)
        def _():
            whole = jnp.concatenate([jnp.ones_like(inner), inner], 0)
            terms(t, (needed_ref[count - 1], own), whole > 0.5)

        @pl.when(lax.rem(count, 2) == 0)
        def _():
            terms(t, (own,), inner > 0.5)

        rows = slice(t * TILE, (t + 1) * TILE)
        cosine = cos_ref[rows, :]
        sine = sin_ref[rows, :]
        for h in range(kv_local * GROUP):
            c, g = h // GROUP, h % GROUP
            x = (dqt[t, c, :, g * TILE : (g + 1) * TILE] * SCALE).T
            x = x * cosine - pltpu.roll(x, HEAD_SIZE // 2, 1) * sine
            dq_ref[rows, h * HEAD_SIZE : (h + 1) * HEAD_SIZE] = x.astype(jnp.bfloat16)


def attention(first_tile, block_mask, prepared, lse, cosine, sine, kv_whole, seg_row):
    qs, dos, turned_q, turned_do, delta = prepared
    q_tiles, kv_local, wide, _ = qs.shape
    tokens = q_tiles * TILE
    vm = pl.BlockSpec(memory_space=pltpu.VMEM)
    sm = pl.BlockSpec(memory_space=pltpu.SMEM)
    return pl.pallas_call(
        attention_kernel,
        out_shape=(
            jax.ShapeDtypeStruct((tokens, kv_local * GROUP * HEAD_SIZE), jnp.bfloat16),
            jax.ShapeDtypeStruct(kv_whole.shape, jnp.float32),
        ),
        in_specs=[sm, sm] + [vm] * 11,
        out_specs=(vm, vm),
        scratch_shapes=[
            pltpu.VMEM((q_tiles, kv_local, 1, wide), jnp.float32),
            pltpu.VMEM((q_tiles, kv_local, HEAD_SIZE, wide), jnp.float32),
            pltpu.SMEM((block_mask.shape[0],), jnp.int32),
        ],
        compiler_params=pltpu.CompilerParams(vmem_limit_bytes=ATTENTION_BYTES),
        name="attention",
    )(
        first_tile, block_mask, qs, dos, turned_q, turned_do, lse, delta, cosine, sine, kv_whole,
        seg_row, seg_row.reshape(tokens, 1),
    )


def project_kernel(
    n_ctx, n, dq_hbm, terms_ref, cos_ref, sin_ref, wq_ref, wk_ref, wv_ref, far_hbm, out_ref,
    wq, wk, wv, acc, send, send_scale, recv, recv_scale,
    far_w, far_dkv, dq_ref, dkv_ref, total, own, near, part, part_scale, far, far_scale,
    w_sem, send_sem, recv_sem, send_scale_sem, recv_scale_sem,
    far_load_sem, far_send_sem, far_recv_sem, raw_sem, dq_sem, own_sem, near_send_sem, near_sem, part_sem, far_sem, part_scale_sem, far_scale_sem,
):
    me = lax.axis_index("tp")
    chips = n_ctx // 2
    place = lax.axis_index("ctx")
    chip, core = place // 2, lax.rem(place, 2)
    sibling = 2 * chip + 1 - core
    tokens, kv_width = dkv_ref.shape
    kv_half = kv_width // 2
    group = tokens // 8
    chunk_rows = out_ref.shape[0]
    sub_rows = acc.shape[0]
    subs = chunk_rows // sub_rows
    steps = 2 * (n - 1) * subs
    is_end, is_next, mate = line_ends(me, n)

    def plan(i):
        way = lax.rem(i, 2)
        rightward = jnp.where(me < n // 2, 1 - way, way)
        sub = lax.rem(i // 2, subs)
        step = i // (2 * subs)
        chunk = jnp.where(rightward == 1, n - 1 - step, step)
        active = jnp.where(rightward == 1, chunk > me, chunk < me)
        early = active & is_end & (step == 0)
        late = active & jnp.logical_not(early)
        joined = is_next & (step == 0) & (rightward == jnp.where(me == 1, 1, 0))
        return rightward, chunk, sub, early, late, joined

    def weight_copies(chunk, sub):
        at = chunk * subs + sub
        rows = pl.ds(pl.multiple_of(at * sub_rows, sub_rows), sub_rows)
        return [
            pltpu.make_async_copy(src.at[rows, :], dst.at[rows, :], w_sem.at[j, at])
            for j, (src, dst) in enumerate(((wq_ref, wq), (wk_ref, wk), (wv_ref, wv)))
        ]

    def remote(rightward, chunk, sub):
        slot = chunk * subs + sub
        to = jnp.where(rightward == 1, jnp.minimum(me + 1, n - 1), jnp.maximum(me - 1, 0))
        return [
            pltpu.make_async_remote_copy(
                src_ref=s.at[slot],
                dst_ref=r.at[rightward, slot],
                send_sem=ss.at[slot],
                recv_sem=rs.at[rightward, slot],
                device_id={"tp": to},
                device_id_type=MESH,
            )
            for s, r, ss, rs in (
                (send, recv, send_sem, recv_sem),
                (send_scale, recv_scale, send_scale_sem, recv_scale_sem),
            )
        ]

    def own_term(chunk, sub):
        for copy in weight_copies(chunk, sub):
            copy.wait()
        at = chunk * subs + sub
        rows = pl.ds(pl.multiple_of(at * sub_rows, sub_rows), sub_rows)
        half = wk.shape[1]
        contract = ((1,), (1,))
        total = dot(wq[rows, :], dq_ref[...], contract)
        total = total + dot(wk[rows, :], dkv_ref[:, :half], contract)
        acc[...] = total + dot(wv[rows, :], dkv_ref[:, half:], contract)

    def add_received(rightward, chunk, sub):
        for copy in remote(rightward, chunk, sub):
            copy.wait_recv()
        slot = chunk * subs + sub
        scale = recv_scale[rightward, slot, 0:1, :]
        acc[...] += recv[rightward, slot].astype(jnp.int32).astype(jnp.float32) * scale

    dq_load = pltpu.make_async_copy(dq_hbm, dq_ref, dq_sem.at[0])
    dq_load.start()

    @pl.loop(0, steps)
    def _(i):
        _, chunk, sub, early, late, _ = plan(i)

        @pl.when(early)
        def _():
            weight_copies(chunk, sub)[0].start()

        @pl.when(late)
        def _():
            for copy in weight_copies(chunk, sub):
                copy.start()

    @pl.loop(0, subs)
    def _(sub):
        for copy in weight_copies(me, sub):
            copy.start()

    barrier = pltpu.get_barrier_semaphore()

    @pl.when(me > 0)
    def _():
        pl.semaphore_signal(barrier, inc=1, device_id={"tp": jnp.maximum(me - 1, 0)}, device_id_type=MESH)

    @pl.when(me < n - 1)
    def _():
        pl.semaphore_signal(barrier, inc=1, device_id={"tp": jnp.minimum(me + 1, n - 1)}, device_id_type=MESH)

    for away in range(1, chips):
        other = 2 * lax.rem(chip + away, chips) + core
        pl.semaphore_signal(barrier, inc=1, device_id={"ctx": other}, device_id_type=MESH)
    pl.semaphore_signal(barrier, inc=1, device_id={"ctx": sibling}, device_id_type=MESH)
    peers = jnp.where(me > 0, 1, 0) + jnp.where(me < n - 1, 1, 0) + chips
    pl.semaphore_wait(barrier, peers)

    def token_rows(block):
        return pl.ds(pl.multiple_of(block * tokens, tokens), tokens)

    def load_own(j):
        return pltpu.make_async_copy(terms_ref.at[token_rows(2 * j + core), :], own.at[j], own_sem.at[j])

    def to_sibling(j):
        return pltpu.make_async_remote_copy(
            src_ref=terms_ref.at[token_rows(2 * j + 1 - core), :],
            dst_ref=near.at[j],
            send_sem=near_send_sem.at[j],
            recv_sem=near_sem.at[j],
            device_id={"ctx": sibling},
            device_id_type=MESH,
        )

    def to_owner(source, j):
        return [
            pltpu.make_async_remote_copy(
                src_ref=p.at[j],
                dst_ref=f.at[source],
                send_sem=ps.at[j],
                recv_sem=fs.at[source],
                device_id={"ctx": 2 * j + core},
                device_id_type=MESH,
            )
            for p, f, ps, fs in (
                (part, far, part_sem, far_sem),
                (part_scale, far_scale, part_scale_sem, far_scale_sem),
            )
        ]

    @pl.loop(0, chip + 1)
    def _(j):
        to_sibling(j).start()
        load_own(j).start()

    far_half = far_w.shape[1] // 2
    mine = pl.ds(pl.multiple_of(core * far_half, far_half), far_half)
    far_loads = [
        pltpu.make_async_copy(far_hbm.at[j, mine, :], far_w.at[j, mine, :], far_load_sem.at[j])
        for j in range(2)
    ]
    far_sends = [
        pltpu.make_async_remote_copy(
            src_ref=far_hbm.at[j, mine, :],
            dst_ref=far_w.at[j, mine, :],
            send_sem=far_send_sem.at[j],
            recv_sem=far_recv_sem.at[j],
            device_id={"ctx": sibling},
            device_id_type=MESH,
        )
        for j in range(2)
    ]
    raw = pltpu.make_async_remote_copy(
        src_ref=dkv_ref,
        dst_ref=far_dkv,
        send_sem=raw_sem.at[0],
        recv_sem=raw_sem.at[1],
        device_id={"tp": mate},
        device_id_type=MESH,
    )

    @pl.when(is_next)
    def _():
        for copy in far_loads + far_sends:
            copy.start()

    def send_coded(rightward, chunk, sub):
        slot = chunk * subs + sub
        largest = jnp.maximum(jnp.max(jnp.abs(acc[...]), axis=0, keepdims=True), 1e-30)
        send_scale[slot] = jnp.broadcast_to(largest * (1.0 / 32767.0), send_scale.shape[1:])
        coded = jnp.round(acc[...] * (32767.0 / largest))
        send[slot] = coded.astype(jnp.int32).astype(jnp.int16)
        for copy in remote(rightward, chunk, sub):
            copy.start()

    def query_parts(first, last):
        @pl.when(is_end)
        def _():
            @pl.loop(first, last)
            def _(sub):
                chunk = jnp.where(me == 0, n - 1, 0)
                weight_copies(chunk, sub)[0].wait()
                rows = pl.ds(pl.multiple_of((chunk * subs + sub) * sub_rows, sub_rows), sub_rows)
                acc[...] = dot(wq[rows, :], dq_ref[...], ((1,), (1,)))
                send_coded(jnp.where(me == 0, 1, 0), chunk, sub)

    dq_load.wait()
    query_parts(0, subs // 2)

    @pl.loop(0, chip)
    def _(j):
        load_own(j).wait()
        to_sibling(j).wait_recv()
        for r in range(8):
            rows = slice(r * group, (r + 1) * group)
            x = own[j, rows, :] + near[j, rows, :]
            largest = jnp.maximum(jnp.max(jnp.abs(x), axis=0, keepdims=True), 1e-30)
            part_scale[j, r : r + 1, :] = largest * (1.0 / 32767.0)
            part[j, rows, :] = jnp.round(x * (32767.0 / largest)).astype(jnp.int32).astype(jnp.int16)
        for copy in to_owner(chip, j):
            copy.start()

    query_parts(subs // 2, subs)
    load_own(chip).wait()
    to_sibling(chip).wait_recv()
    total[...] = own[chip] + near[chip]

    @pl.loop(chip + 1, chips)
    def _(j):
        for copy in to_owner(j, chip):
            copy.wait_recv()
        for r in range(8):
            rows = slice(r * group, (r + 1) * group)
            x = far[j, rows, :].astype(jnp.int32).astype(jnp.float32)
            total[rows, :] += x * far_scale[j, r : r + 1, :]

    for c in range(kv_half // HEAD_SIZE):
        cols = slice(c * HEAD_SIZE, (c + 1) * HEAD_SIZE)
        x = total[:, cols] * SCALE
        x = x * cos_ref[...] - pltpu.roll(x, HEAD_SIZE // 2, 1) * sin_ref[...]
        dkv_ref[:, cols] = x.astype(jnp.bfloat16)
    dkv_ref[:, kv_half:] = total[:, kv_half:].astype(jnp.bfloat16)

    @pl.when(is_end)
    def _():
        raw.start()

    @pl.when(is_next)
    def _():
        for copy in far_loads:
            copy.wait()
        for copy in far_sends:
            copy.wait_recv()
            copy.wait_send()
        raw.wait_recv()

    @pl.loop(0, chip + 1)
    def _(j):
        to_sibling(j).wait_send()

    @pl.loop(0, chip)
    def _(j):
        for copy in to_owner(chip, j):
            copy.wait_send()

    @pl.loop(0, steps)
    def _(i):
        rightward, chunk, sub, _, late, joined = plan(i)

        @pl.when(late)
        def _():
            own_term(chunk, sub)

            @pl.when(jnp.where(rightward == 1, me > 0, me < n - 1))
            def _():
                add_received(rightward, chunk, sub)

            @pl.when(joined)
            def _():
                rows = pl.ds(pl.multiple_of(sub * sub_rows, sub_rows), sub_rows)
                extra = dot(far_w[0, rows, :], far_dkv[:, :kv_half], ((1,), (1,)))
                acc[...] += extra + dot(far_w[1, rows, :], far_dkv[:, kv_half:], ((1,), (1,)))

            send_coded(rightward, chunk, sub)

    @pl.loop(0, subs)
    def _(sub):
        own_term(me, sub)

        @pl.when(me > 0)
        def _():
            add_received(1, me, sub)

        @pl.when(me < n - 1)
        def _():
            add_received(0, me, sub)

        rows = pl.ds(pl.multiple_of(sub * sub_rows, sub_rows), sub_rows)
        out_ref[rows, :] = acc[...].astype(jnp.bfloat16)

    @pl.loop(0, steps)
    def _(i):
        rightward, chunk, sub, early, late, _ = plan(i)

        @pl.when(early | late)
        def _():
            for copy in remote(rightward, chunk, sub):
                copy.wait_send()

    @pl.when(is_end)
    def _():
        raw.wait_send()


def project(n_ctx, n, dq, terms, cosine, sine, w_query, key_weight, value_weight, far_weight):
    tokens = dq.shape[0]
    kv_width = terms.shape[1]
    chips = n_ctx // 2
    width = w_query.shape[0]
    chunk_rows = width // n
    sub_rows = 320 if chunk_rows % 320 == 0 else chunk_rows
    slots = width // sub_rows
    vm = pl.BlockSpec(memory_space=pltpu.VMEM)
    hbm = pl.BlockSpec(memory_space=pl.ANY)
    dma = pltpu.SemaphoreType.DMA
    return pl.pallas_call(
        functools.partial(project_kernel, n_ctx, n),
        out_shape=jax.ShapeDtypeStruct((chunk_rows, tokens), jnp.bfloat16),
        in_specs=[hbm, hbm, vm, vm, hbm, hbm, hbm, hbm],
        out_specs=vm,
        scratch_shapes=[
            pltpu.VMEM(w_query.shape, jnp.bfloat16),
            pltpu.VMEM(key_weight.shape, jnp.bfloat16),
            pltpu.VMEM(value_weight.shape, jnp.bfloat16),
            pltpu.VMEM((sub_rows, tokens), jnp.float32),
            pltpu.VMEM((slots, sub_rows, tokens), jnp.int16),
            pltpu.VMEM((slots, 8, tokens), jnp.float32),
            pltpu.VMEM((2, slots, sub_rows, tokens), jnp.int16),
            pltpu.VMEM((2, slots, 8, tokens), jnp.float32),
            pltpu.VMEM(far_weight.shape, jnp.bfloat16),
            pltpu.VMEM((tokens, kv_width), jnp.bfloat16),
            pltpu.VMEM(dq.shape, jnp.bfloat16),
            pltpu.VMEM((tokens, kv_width), jnp.bfloat16),
            pltpu.VMEM((tokens, kv_width), jnp.float32),
            pltpu.VMEM((chips, tokens, kv_width), jnp.float32),
            pltpu.VMEM((chips, tokens, kv_width), jnp.float32),
            pltpu.VMEM((chips, tokens, kv_width), jnp.int16),
            pltpu.VMEM((chips, 8, kv_width), jnp.float32),
            pltpu.VMEM((chips, tokens, kv_width), jnp.int16),
            pltpu.VMEM((chips, 8, kv_width), jnp.float32),
            dma((3, slots)),
            dma((slots,)),
            dma((2, slots)),
            dma((slots,)),
            dma((2, slots)),
        ]
        + [dma((2,))] * 4
        + [dma((1,))]
        + [dma((chips,))] * 7,
        compiler_params=pltpu.CompilerParams(
            collective_id=2, has_side_effects=True, vmem_limit_bytes=PROJECT_BYTES
        ),
        name="project",
    )(dq, terms, cosine, sine, w_query, key_weight, value_weight, far_weight)


def local(
    n_ctx,
    n_tp,
    query,
    key_projected,
    value,
    attention_output,
    output_gradient,
    lse,
    block_mask,
    positions,
    segments,
    w_query,
    key_weight,
    value_weight,
):
    tok_rows = query.shape[0]
    q_start = lax.axis_index("ctx") * tok_rows
    cosine, sine = rope_tables(positions, HEAD_SIZE)
    kv_blocks, *prepared, far_weight = gather(
        n_ctx, n_tp, key_projected, value, query, output_gradient, attention_output, cosine, sine,
        key_weight, value_weight,
    )
    kv_whole = kv_blocks.reshape(n_ctx * tok_rows, kv_blocks.shape[-1])
    seg_row = lax.dynamic_slice_in_dim(segments, q_start, tok_rows).reshape(1, tok_rows)
    first_tile = (q_start // TILE).astype(jnp.int32).reshape(1)
    query_grad, terms = attention(
        first_tile, block_mask, prepared, lse, cosine, sine, kv_whole, seg_row
    )
    return project(
        n_ctx, n_tp, query_grad, terms, cosine, sine, w_query, key_weight, value_weight, far_weight
    )


def solution(mesh):
    in_specs = (
        P("ctx", "tp"),
        P("ctx", "tp"),
        P("ctx", "tp"),
        P("ctx", "tp"),
        P("ctx", "tp"),
        P("tp", "ctx"),
        P(),
        P("ctx"),
        P(),
        P(None, "tp"),
        P(None, "tp"),
        P(None, "tp"),
    )
    out_specs = P("tp", "ctx")
    body = functools.partial(local, mesh.shape["ctx"], mesh.shape["tp"])
    return jax.shard_map(body, mesh=mesh, in_specs=in_specs, out_specs=out_specs, check_vma=False)
```

```python
import functools

import jax
import jax.numpy as jnp
from jax import lax
from jax.experimental import pallas as pl
from jax.experimental.pallas import tpu as pltpu
from jax.sharding import PartitionSpec as P

QUERY_HEADS = 40
KEY_VALUE_HEADS = 8
HEAD_SIZE = 128
TILE = 128
GROUP = QUERY_HEADS // KEY_VALUE_HEADS
SCALE = HEAD_SIZE ** (-0.5)
MESH = pl.DeviceIdType.MESH
PROJECT_BYTES = 60 * 1024 * 1024
ATTENTION_BYTES = 56 * 1024 * 1024

rope_base = 1000000.0


def rope_tables(positions, head_dim):
    half = head_dim // 2
    exponent = jnp.arange(half).astype(jnp.float32) * (2.0 / head_dim)
    inverse = jnp.power(jnp.float32(rope_base), -exponent)
    angles = positions.astype(jnp.float32)[:, None] * inverse[None, :]
    cosine_table = jnp.cos(angles)
    sine_table = jnp.sin(angles)
    return (
        jnp.concatenate([cosine_table, cosine_table], 1),
        jnp.concatenate([-sine_table, sine_table], 1),
    )


def dot(a, b, dims=((1,), (0,))):
    return lax.dot_general(a, b, (dims, ((), ())), preferred_element_type=jnp.float32)


def line_ends(at, n):
    is_end = (at == 0) | (at == n - 1)
    is_next = (at == 1) | (at == n - 2)
    mate = jnp.where(at == 0, 1, jnp.where(at == n - 1, n - 2, jnp.where(at == 1, 0, n - 1)))
    return is_end, is_next, mate


def gather_kernel(
    n, n_tp, kp_hbm, v_hbm, q_hbm, do_hbm, ao_hbm, cos_ref, sin_ref, wk_hbm, wv_hbm,
    kv_ref, qs_ref, dos_ref, qt_ref, dot_ref, delta_ref, far_ref,
    kp_ref, q_ref, do_ref, ao_ref, load_sem, far_send_sem, far_recv_sem,
    send_sem, recv_sem, pass_sem, pass_recv_sem,
):
    me = lax.axis_index("ctx")
    chip, core = me // 2, lax.rem(me, 2)
    sibling = 2 * chip + 1 - core
    chips = n // 2
    tokens, kv_cols = kp_ref.shape
    heads = q_ref.shape[1] // HEAD_SIZE
    q_tiles = tokens // TILE
    loads = [
        pltpu.make_async_copy(src, dst, load_sem.at[j])
        for j, (src, dst) in enumerate(
            (
                (kp_hbm, kp_ref),
                (v_hbm, kv_ref.at[me, :, pl.ds(kv_cols, kv_cols)]),
                (q_hbm, q_ref),
                (do_hbm, do_ref),
                (ao_hbm, ao_ref),
            )
        )
    ]
    for copy in loads:
        copy.start()

    barrier = pltpu.get_barrier_semaphore()
    for away in range(1, chips):
        other = 2 * lax.rem(chip + away, chips) + core
        pl.semaphore_signal(barrier, inc=1, device_id={"ctx": other}, device_id_type=MESH)
    pl.semaphore_signal(barrier, inc=1, device_id={"ctx": sibling}, device_id_type=MESH)

    line = lax.axis_index("tp")
    is_end, is_next, mate = line_ends(line, n_tp)
    half = far_ref.shape[1] // 2
    chunk = jnp.where(line == 0, n_tp - 1, 0)

    def far_weights():
        rows = pl.ds(pl.multiple_of(chunk * 2 * half + core * half, half), half)
        there = pl.ds(pl.multiple_of(core * half, half), half)
        return [
            pltpu.make_async_remote_copy(
                src_ref=src.at[rows, :],
                dst_ref=far_ref.at[j, there, :],
                send_sem=far_send_sem.at[j],
                recv_sem=far_recv_sem.at[j],
                device_id={"tp": mate},
                device_id_type=MESH,
            )
            for j, src in enumerate((wk_hbm, wv_hbm))
        ]

    @pl.when(is_end | is_next)
    def _():
        pl.semaphore_signal(barrier, inc=1, device_id={"tp": mate}, device_id_type=MESH)

    loads[0].wait()
    for c in range(kv_cols // HEAD_SIZE):
        cols = slice(c * HEAD_SIZE, (c + 1) * HEAD_SIZE)
        x = kp_ref[:, cols].astype(jnp.float32)
        x = x * cos_ref[...] + pltpu.roll(x, HEAD_SIZE // 2, 1) * sin_ref[...]
        kv_ref[me, :, cols] = x.astype(jnp.bfloat16)
    loads[1].wait()

    def direct(source, target):
        slot = 2 * source + core
        return pltpu.make_async_remote_copy(
            src_ref=kv_ref.at[slot],
            dst_ref=kv_ref.at[slot],
            send_sem=send_sem.at[target],
            recv_sem=recv_sem.at[source],
            device_id={"ctx": 2 * target + core},
            device_id_type=MESH,
        )

    def handed(source, from_core):
        slot = 2 * source + from_core
        return pltpu.make_async_remote_copy(
            src_ref=kv_ref.at[slot],
            dst_ref=kv_ref.at[slot],
            send_sem=pass_sem.at[source],
            recv_sem=pass_recv_sem.at[source],
            device_id={"ctx": sibling},
            device_id_type=MESH,
        )

    pl.semaphore_wait(barrier, chips + jnp.where(is_end | is_next, 1, 0))
    for away in range(chips - 1, 0, -1):

        @pl.when(chip + away < chips)
        def _():
            direct(chip, jnp.minimum(chip + away, chips - 1)).start()

    handed(chip, core).start()

    @pl.when(is_end)
    def _():
        for copy in far_weights():
            copy.start()

    for copy in loads[2:]:
        copy.wait()

    @pl.loop(0, q_tiles * heads)
    def _(i):
        t, h = i // heads, lax.rem(i, heads)
        c, g = h // GROUP, lax.rem(h, GROUP)
        rows = pl.ds(pl.multiple_of(t * TILE, TILE), TILE)
        cols = pl.ds(pl.multiple_of(h * HEAD_SIZE, HEAD_SIZE), HEAD_SIZE)
        part = pl.ds(pl.multiple_of(g * TILE, TILE), TILE)
        x = q_ref[rows, cols].astype(jnp.float32)
        x = x * cos_ref[rows, :] + pltpu.roll(x, HEAD_SIZE // 2, 1) * sin_ref[rows, :]
        xb = x.astype(jnp.bfloat16)
        qs_ref[t, c, part, :] = xb
        qt_ref[t, c, :, part] = xb.astype(jnp.float32).T.astype(jnp.bfloat16)
        y = do_ref[rows, cols]
        dos_ref[t, c, part, :] = y
        y_turned = y.astype(jnp.float32).T
        dot_ref[t, c, :, part] = y_turned.astype(jnp.bfloat16)
        o_turned = ao_ref[rows, cols].astype(jnp.float32).T
        delta_ref[t, c, :, part] = jnp.sum(y_turned * o_turned, axis=0, keepdims=True)

    for away in range(1, chips):

        @pl.when(chip - away >= 0)
        def _():
            source = jnp.maximum(chip - away, 0)
            direct(source, chip).wait_recv()
            handed(source, core).start()

    for away in range(chips):

        @pl.when(chip - away >= 0)
        def _():
            source = jnp.maximum(chip - away, 0)
            handed(source, 1 - core).wait_recv()
            handed(source, core).wait_send()

    for away in range(1, chips):

        @pl.when(chip + away < chips)
        def _():
            direct(chip, jnp.minimum(chip + away, chips - 1)).wait_send()

    @pl.when(is_next)
    def _():
        for copy in far_weights():
            copy.wait_recv()

    @pl.when(is_end)
    def _():
        for copy in far_weights():
            copy.wait_send()


def gather(n, n_tp, key_projected, value, query, grad, attention_output, cosine, sine, key_weight, value_weight):
    tokens, kv_cols = key_projected.shape
    kv_local = kv_cols // HEAD_SIZE
    q_tiles = tokens // TILE
    wide = GROUP * TILE
    vm = pl.BlockSpec(memory_space=pltpu.VMEM)
    hbm = pl.BlockSpec(memory_space=pltpu.HBM)
    dma = pltpu.SemaphoreType.DMA
    stacked = jax.ShapeDtypeStruct((q_tiles, kv_local, wide, HEAD_SIZE), jnp.bfloat16)
    turned = jax.ShapeDtypeStruct((q_tiles, kv_local, HEAD_SIZE, wide), jnp.bfloat16)
    return pl.pallas_call(
        functools.partial(gather_kernel, n, n_tp),
        out_shape=(
            jax.ShapeDtypeStruct((n, tokens, 2 * kv_cols), jnp.bfloat16),
            stacked,
            stacked,
            turned,
            turned,
            jax.ShapeDtypeStruct((q_tiles, kv_local, 1, wide), jnp.float32),
            jax.ShapeDtypeStruct((2, key_weight.shape[0] // n_tp, kv_cols), jnp.bfloat16),
        ),
        in_specs=[hbm] * 5 + [vm, vm, hbm, hbm],
        out_specs=(vm,) * 6 + (pl.BlockSpec(memory_space=pl.ANY),),
        scratch_shapes=[pltpu.VMEM(key_projected.shape, jnp.bfloat16)]
        + [pltpu.VMEM(query.shape, jnp.bfloat16)] * 3
        + [dma((5,)), dma((2,)), dma((2,))]
        + [dma((n // 2,))] * 4,
        compiler_params=pltpu.CompilerParams(
            collective_id=1, has_side_effects=True, vmem_limit_bytes=ATTENTION_BYTES
        ),
        name="gather",
    )(key_projected, value, query, grad, attention_output, cosine, sine, key_weight, value_weight)


def attention_kernel(
    start_ref, mask_ref, qs, dos, qt_s, dot_s, lse_ref, delta_s, cos_ref, sin_ref, kv_ref, segq_ref, segk_ref,
    dq_ref, dkv_ref, lse_s, dqt, needed_ref,
):
    tokens = dq_ref.shape[0]
    kv_local = kv_ref.shape[1] // (2 * HEAD_SIZE)
    q_tiles = tokens // TILE
    first_tile = start_ref[0]
    dkv_ref[...] = jnp.zeros_like(dkv_ref)
    dqt[...] = jnp.zeros_like(dqt)
    for t in range(q_tiles):
        for h in range(kv_local * GROUP):
            c, g = h // GROUP, h % GROUP
            lse_s[t, c, :, g * TILE : (g + 1) * TILE] = lse_ref[h : h + 1, t * TILE : (t + 1) * TILE]

    def terms(t, k_tiles, allowed):
        spans = [pl.ds(pl.multiple_of(k * TILE, TILE), TILE) for k in k_tiles]
        for c in range(kv_local):
            key_cols = slice(c * HEAD_SIZE, (c + 1) * HEAD_SIZE)
            val_cols = slice((kv_local + c) * HEAD_SIZE, (kv_local + c + 1) * HEAD_SIZE)
            k = jnp.concatenate([kv_ref[span, key_cols] for span in spans], 0)
            v = jnp.concatenate([kv_ref[span, val_cols] for span in spans], 0)
            scores = dot(k, qt_s[t, c]) * SCALE
            probs = jnp.exp(scores - lse_s[t, c])
            if allowed is not None:
                probs = jnp.where(allowed, probs, 0.0)
            dscore = probs * (dot(v, dot_s[t, c]) - delta_s[t, c])
            pb = probs.astype(jnp.bfloat16)
            db = dscore.astype(jnp.bfloat16)
            dk = dot(db, qs[t, c])
            dv = dot(pb, dos[t, c])
            for j, span in enumerate(spans):
                dkv_ref[span, key_cols] += dk[j * TILE : (j + 1) * TILE]
                dkv_ref[span, val_cols] += dv[j * TILE : (j + 1) * TILE]
            kt = k.astype(jnp.float32).T.astype(jnp.bfloat16)
            dqt[t, c] += dot(kt, db)

    for t in range(q_tiles):
        own = first_tile + t

        def note(k_tile, count):
            needed_ref[count] = k_tile
            return count + jnp.where(mask_ref[own, k_tile] > 0, 1, 0)

        count = lax.fori_loop(0, own, note, jnp.int32(0))

        @pl.loop(0, count // 2)
        def _(i):
            terms(t, (needed_ref[2 * i], needed_ref[2 * i + 1]), None)

        row = lax.broadcasted_iota(jnp.int32, (TILE, TILE), 0)
        col = lax.broadcasted_iota(jnp.int32, (TILE, TILE), 1)
        seg_k = segk_ref[t * TILE : (t + 1) * TILE, :]
        seg_q = segq_ref[:, t * TILE : (t + 1) * TILE]
        inner = jnp.where((row <= col) & (seg_k == seg_q), 1.0, 0.0)
        inner = jnp.concatenate([inner] * GROUP, 1)

        @pl.when(lax.rem(count, 2) == 1)
        def _():
            whole = jnp.concatenate([jnp.ones_like(inner), inner], 0)
            terms(t, (needed_ref[count - 1], own), whole > 0.5)

        @pl.when(lax.rem(count, 2) == 0)
        def _():
            terms(t, (own,), inner > 0.5)

        rows = slice(t * TILE, (t + 1) * TILE)
        cosine = cos_ref[rows, :]
        sine = sin_ref[rows, :]
        for h in range(kv_local * GROUP):
            c, g = h // GROUP, h % GROUP
            x = (dqt[t, c, :, g * TILE : (g + 1) * TILE] * SCALE).T
            x = x * cosine - pltpu.roll(x, HEAD_SIZE // 2, 1) * sine
            dq_ref[rows, h * HEAD_SIZE : (h + 1) * HEAD_SIZE] = x.astype(jnp.bfloat16)


def attention(first_tile, block_mask, prepared, lse, cosine, sine, kv_whole, seg_row):
    qs, dos, turned_q, turned_do, delta = prepared
    q_tiles, kv_local, wide, _ = qs.shape
    tokens = q_tiles * TILE
    vm = pl.BlockSpec(memory_space=pltpu.VMEM)
    sm = pl.BlockSpec(memory_space=pltpu.SMEM)
    return pl.pallas_call(
        attention_kernel,
        out_shape=(
            jax.ShapeDtypeStruct((tokens, kv_local * GROUP * HEAD_SIZE), jnp.bfloat16),
            jax.ShapeDtypeStruct(kv_whole.shape, jnp.float32),
        ),
        in_specs=[sm, sm] + [vm] * 11,
        out_specs=(vm, vm),
        scratch_shapes=[
            pltpu.VMEM((q_tiles, kv_local, 1, wide), jnp.float32),
            pltpu.VMEM((q_tiles, kv_local, HEAD_SIZE, wide), jnp.float32),
            pltpu.SMEM((block_mask.shape[0],), jnp.int32),
        ],
        compiler_params=pltpu.CompilerParams(vmem_limit_bytes=ATTENTION_BYTES),
        name="attention",
    )(
        first_tile, block_mask, qs, dos, turned_q, turned_do, lse, delta, cosine, sine, kv_whole,
        seg_row, seg_row.reshape(tokens, 1),
    )


def project_kernel(
    n_ctx, n, dq_hbm, terms_ref, cos_ref, sin_ref, wq_ref, wk_ref, wv_ref, far_hbm, out_ref,
    wq, wk, wv, acc, send, send_scale, recv, recv_scale,
    far_w, far_dkv, dq_ref, dq_turned, query_part, dkv_ref, total, own, near, part, part_scale, far, far_scale,
    w_sem, send_sem, recv_sem, send_scale_sem, recv_scale_sem,
    far_load_sem, far_send_sem, far_recv_sem, raw_sem, dq_sem, own_sem, near_send_sem, near_sem, part_sem, far_sem, part_scale_sem, far_scale_sem,
):
    me = lax.axis_index("tp")
    chips = n_ctx // 2
    place = lax.axis_index("ctx")
    chip, core = place // 2, lax.rem(place, 2)
    sibling = 2 * chip + 1 - core
    kv_width, tokens = dkv_ref.shape
    kv_half = kv_width // 2
    group = tokens // 8
    chunk_rows = out_ref.shape[0]
    sub_rows = acc.shape[0]
    subs = chunk_rows // sub_rows
    steps = 2 * (n - 1) * subs
    is_end, is_next, mate = line_ends(me, n)

    def plan(i):
        way = lax.rem(i, 2)
        rightward = jnp.where(me < n // 2, 1 - way, way)
        sub = lax.rem(i // 2, subs)
        step = i // (2 * subs)
        chunk = jnp.where(rightward == 1, n - 1 - step, step)
        active = jnp.where(rightward == 1, chunk > me, chunk < me)
        early = active & is_end & (step == 0)
        late = active & jnp.logical_not(early)
        joined = is_next & (step == 0) & (rightward == jnp.where(me == 1, 1, 0))
        return rightward, chunk, sub, early, late, joined

    def weight_copies(chunk, sub):
        at = chunk * subs + sub
        rows = pl.ds(pl.multiple_of(at * sub_rows, sub_rows), sub_rows)
        return [
            pltpu.make_async_copy(src.at[rows, :], dst.at[rows, :], w_sem.at[j, at])
            for j, (src, dst) in enumerate(((wq_ref, wq), (wk_ref, wk), (wv_ref, wv)))
        ]

    def remote(rightward, chunk, sub):
        slot = chunk * subs + sub
        to = jnp.where(rightward == 1, jnp.minimum(me + 1, n - 1), jnp.maximum(me - 1, 0))
        return [
            pltpu.make_async_remote_copy(
                src_ref=s.at[slot],
                dst_ref=r.at[rightward, slot],
                send_sem=ss.at[slot],
                recv_sem=rs.at[rightward, slot],
                device_id={"tp": to},
                device_id_type=MESH,
            )
            for s, r, ss, rs in (
                (send, recv, send_sem, recv_sem),
                (send_scale, recv_scale, send_scale_sem, recv_scale_sem),
            )
        ]

    def own_term(chunk, sub):
        for copy in weight_copies(chunk, sub)[1:]:
            copy.wait()
        at = chunk * subs + sub
        rows = pl.ds(pl.multiple_of(at * sub_rows, sub_rows), sub_rows)
        half = wk.shape[1]
        term = query_part[rows, :] + dot(wk[rows, :], dkv_ref[:half, :])
        acc[...] = term + dot(wv[rows, :], dkv_ref[half:, :])

    def add_received(rightward, chunk, sub):
        for copy in remote(rightward, chunk, sub):
            copy.wait_recv()
        slot = chunk * subs + sub
        scale = recv_scale[rightward, slot, 0:1, :]
        acc[...] += recv[rightward, slot].astype(jnp.int32).astype(jnp.float32) * scale

    dq_load = pltpu.make_async_copy(dq_hbm, dq_ref, dq_sem.at[0])
    dq_load.start()

    @pl.loop(0, steps)
    def _(i):
        _, chunk, sub, early, late, _ = plan(i)

        @pl.when(early)
        def _():
            weight_copies(chunk, sub)[0].start()

        @pl.when(late)
        def _():
            for copy in weight_copies(chunk, sub):
                copy.start()

    @pl.loop(0, subs)
    def _(sub):
        for copy in weight_copies(me, sub):
            copy.start()

    barrier = pltpu.get_barrier_semaphore()

    @pl.when(me > 0)
    def _():
        pl.semaphore_signal(barrier, inc=1, device_id={"tp": jnp.maximum(me - 1, 0)}, device_id_type=MESH)

    @pl.when(me < n - 1)
    def _():
        pl.semaphore_signal(barrier, inc=1, device_id={"tp": jnp.minimum(me + 1, n - 1)}, device_id_type=MESH)

    for away in range(1, chips):
        other = 2 * lax.rem(chip + away, chips) + core
        pl.semaphore_signal(barrier, inc=1, device_id={"ctx": other}, device_id_type=MESH)
    pl.semaphore_signal(barrier, inc=1, device_id={"ctx": sibling}, device_id_type=MESH)
    peers = jnp.where(me > 0, 1, 0) + jnp.where(me < n - 1, 1, 0) + chips
    pl.semaphore_wait(barrier, peers)

    def token_rows(block):
        return pl.ds(pl.multiple_of(block * tokens, tokens), tokens)

    def load_own(j):
        return pltpu.make_async_copy(terms_ref.at[token_rows(2 * j + core), :], own.at[j], own_sem.at[j])

    def to_sibling(j):
        return pltpu.make_async_remote_copy(
            src_ref=terms_ref.at[token_rows(2 * j + 1 - core), :],
            dst_ref=near.at[j],
            send_sem=near_send_sem.at[j],
            recv_sem=near_sem.at[j],
            device_id={"ctx": sibling},
            device_id_type=MESH,
        )

    def to_owner(source, j):
        return [
            pltpu.make_async_remote_copy(
                src_ref=p.at[j],
                dst_ref=f.at[source],
                send_sem=ps.at[j],
                recv_sem=fs.at[source],
                device_id={"ctx": 2 * j + core},
                device_id_type=MESH,
            )
            for p, f, ps, fs in (
                (part, far, part_sem, far_sem),
                (part_scale, far_scale, part_scale_sem, far_scale_sem),
            )
        ]

    @pl.loop(0, chip + 1)
    def _(j):
        to_sibling(j).start()
        load_own(j).start()

    far_half = far_w.shape[1] // 2
    mine = pl.ds(pl.multiple_of(core * far_half, far_half), far_half)
    far_loads = [
        pltpu.make_async_copy(far_hbm.at[j, mine, :], far_w.at[j, mine, :], far_load_sem.at[j])
        for j in range(2)
    ]
    far_sends = [
        pltpu.make_async_remote_copy(
            src_ref=far_hbm.at[j, mine, :],
            dst_ref=far_w.at[j, mine, :],
            send_sem=far_send_sem.at[j],
            recv_sem=far_recv_sem.at[j],
            device_id={"ctx": sibling},
            device_id_type=MESH,
        )
        for j in range(2)
    ]
    raw = pltpu.make_async_remote_copy(
        src_ref=dkv_ref,
        dst_ref=far_dkv,
        send_sem=raw_sem.at[0],
        recv_sem=raw_sem.at[1],
        device_id={"tp": mate},
        device_id_type=MESH,
    )

    @pl.when(is_next)
    def _():
        for copy in far_loads + far_sends:
            copy.start()

    def send_coded(rightward, chunk, sub):
        slot = chunk * subs + sub
        largest = jnp.maximum(jnp.max(jnp.abs(acc[...]), axis=0, keepdims=True), 1e-30)
        send_scale[slot] = jnp.broadcast_to(largest * (1.0 / 32767.0), send_scale.shape[1:])
        coded = jnp.round(acc[...] * (32767.0 / largest))
        send[slot] = coded.astype(jnp.int32).astype(jnp.int16)
        for copy in remote(rightward, chunk, sub):
            copy.start()

    def query_parts(first, last):
        @pl.when(is_end)
        def _():
            @pl.loop(first, last)
            def _(sub):
                chunk = jnp.where(me == 0, n - 1, 0)
                weight_copies(chunk, sub)[0].wait()
                rows = pl.ds(pl.multiple_of((chunk * subs + sub) * sub_rows, sub_rows), sub_rows)
                acc[...] = dot(wq[rows, :], dq_turned[...])
                send_coded(jnp.where(me == 0, 1, 0), chunk, sub)

    def own_query(chunk, sub):
        weight_copies(chunk, sub)[0].wait()
        rows = pl.ds(pl.multiple_of((chunk * subs + sub) * sub_rows, sub_rows), sub_rows)
        query_part[rows, :] = dot(wq[rows, :], dq_turned[...])

    dq_load.wait()

    @pl.loop(0, dq_ref.shape[1] // HEAD_SIZE)
    def _(h):
        cols = pl.ds(pl.multiple_of(h * HEAD_SIZE, HEAD_SIZE), HEAD_SIZE)
        dq_turned[cols, :] = dq_ref[:, cols].astype(jnp.float32).T.astype(jnp.bfloat16)

    query_parts(0, subs // 2)

    @pl.loop(0, chip)
    def _(j):
        load_own(j).wait()
        to_sibling(j).wait_recv()
        for r in range(8):
            rows = slice(r * group, (r + 1) * group)
            x = own[j, rows, :] + near[j, rows, :]
            largest = jnp.maximum(jnp.max(jnp.abs(x), axis=0, keepdims=True), 1e-30)
            part_scale[j, r : r + 1, :] = largest * (1.0 / 32767.0)
            part[j, rows, :] = jnp.round(x * (32767.0 / largest)).astype(jnp.int32).astype(jnp.int16)
        for copy in to_owner(chip, j):
            copy.start()

    query_parts(subs // 2, subs)

    @pl.loop(0, steps)
    def _(i):
        _, chunk, sub, _, late, _ = plan(i)

        @pl.when(late)
        def _():
            own_query(chunk, sub)

    @pl.loop(0, subs)
    def _(sub):
        own_query(me, sub)

    load_own(chip).wait()
    to_sibling(chip).wait_recv()
    total[...] = own[chip] + near[chip]

    @pl.loop(chip + 1, chips)
    def _(j):
        for copy in to_owner(j, chip):
            copy.wait_recv()
        for r in range(8):
            rows = slice(r * group, (r + 1) * group)
            x = far[j, rows, :].astype(jnp.int32).astype(jnp.float32)
            total[rows, :] += x * far_scale[j, r : r + 1, :]

    for c in range(kv_half // HEAD_SIZE):
        cols = slice(c * HEAD_SIZE, (c + 1) * HEAD_SIZE)
        x = total[:, cols] * SCALE
        x = x * cos_ref[...] - pltpu.roll(x, HEAD_SIZE // 2, 1) * sin_ref[...]
        dkv_ref[cols, :] = x.T.astype(jnp.bfloat16)
        v_cols = slice(kv_half + c * HEAD_SIZE, kv_half + (c + 1) * HEAD_SIZE)
        dkv_ref[v_cols, :] = total[:, v_cols].T.astype(jnp.bfloat16)

    @pl.when(is_end)
    def _():
        raw.start()

    @pl.when(is_next)
    def _():
        for copy in far_loads:
            copy.wait()
        for copy in far_sends:
            copy.wait_recv()
            copy.wait_send()
        raw.wait_recv()

    @pl.loop(0, chip + 1)
    def _(j):
        to_sibling(j).wait_send()

    @pl.loop(0, chip)
    def _(j):
        for copy in to_owner(chip, j):
            copy.wait_send()

    @pl.loop(0, steps)
    def _(i):
        rightward, chunk, sub, _, late, joined = plan(i)

        @pl.when(late)
        def _():
            own_term(chunk, sub)

            @pl.when(jnp.where(rightward == 1, me > 0, me < n - 1))
            def _():
                add_received(rightward, chunk, sub)

            @pl.when(joined)
            def _():
                rows = pl.ds(pl.multiple_of(sub * sub_rows, sub_rows), sub_rows)
                extra = dot(far_w[0, rows, :], far_dkv[:kv_half, :])
                acc[...] += extra + dot(far_w[1, rows, :], far_dkv[kv_half:, :])

            send_coded(rightward, chunk, sub)

    @pl.loop(0, subs)
    def _(sub):
        own_term(me, sub)

        @pl.when(me > 0)
        def _():
            add_received(1, me, sub)

        @pl.when(me < n - 1)
        def _():
            add_received(0, me, sub)

        rows = pl.ds(pl.multiple_of(sub * sub_rows, sub_rows), sub_rows)
        out_ref[rows, :] = acc[...].astype(jnp.bfloat16)

    @pl.loop(0, steps)
    def _(i):
        rightward, chunk, sub, early, late, _ = plan(i)

        @pl.when(early | late)
        def _():
            for copy in remote(rightward, chunk, sub):
                copy.wait_send()

    @pl.when(is_end)
    def _():
        raw.wait_send()


def project(n_ctx, n, dq, terms, cosine, sine, w_query, key_weight, value_weight, far_weight):
    tokens = dq.shape[0]
    kv_width = terms.shape[1]
    chips = n_ctx // 2
    width = w_query.shape[0]
    chunk_rows = width // n
    sub_rows = 320 if chunk_rows % 320 == 0 else chunk_rows
    slots = width // sub_rows
    vm = pl.BlockSpec(memory_space=pltpu.VMEM)
    hbm = pl.BlockSpec(memory_space=pl.ANY)
    dma = pltpu.SemaphoreType.DMA
    return pl.pallas_call(
        functools.partial(project_kernel, n_ctx, n),
        out_shape=jax.ShapeDtypeStruct((chunk_rows, tokens), jnp.bfloat16),
        in_specs=[hbm, hbm, vm, vm, hbm, hbm, hbm, hbm],
        out_specs=vm,
        scratch_shapes=[
            pltpu.VMEM(w_query.shape, jnp.bfloat16),
            pltpu.VMEM(key_weight.shape, jnp.bfloat16),
            pltpu.VMEM(value_weight.shape, jnp.bfloat16),
            pltpu.VMEM((sub_rows, tokens), jnp.float32),
            pltpu.VMEM((slots, sub_rows, tokens), jnp.int16),
            pltpu.VMEM((slots, 8, tokens), jnp.float32),
            pltpu.VMEM((2, slots, sub_rows, tokens), jnp.int16),
            pltpu.VMEM((2, slots, 8, tokens), jnp.float32),
            pltpu.VMEM(far_weight.shape, jnp.bfloat16),
            pltpu.VMEM((kv_width, tokens), jnp.bfloat16),
            pltpu.VMEM(dq.shape, jnp.bfloat16),
            pltpu.VMEM(dq.shape[::-1], jnp.bfloat16),
            pltpu.VMEM((width, tokens), jnp.float32),
            pltpu.VMEM((kv_width, tokens), jnp.bfloat16),
            pltpu.VMEM((tokens, kv_width), jnp.float32),
            pltpu.VMEM((chips, tokens, kv_width), jnp.float32),
            pltpu.VMEM((chips, tokens, kv_width), jnp.float32),
            pltpu.VMEM((chips, tokens, kv_width), jnp.int16),
            pltpu.VMEM((chips, 8, kv_width), jnp.float32),
            pltpu.VMEM((chips, tokens, kv_width), jnp.int16),
            pltpu.VMEM((chips, 8, kv_width), jnp.float32),
            dma((3, slots)),
            dma((slots,)),
            dma((2, slots)),
            dma((slots,)),
            dma((2, slots)),
        ]
        + [dma((2,))] * 4
        + [dma((1,))]
        + [dma((chips,))] * 7,
        compiler_params=pltpu.CompilerParams(
            collective_id=2, has_side_effects=True, vmem_limit_bytes=PROJECT_BYTES
        ),
        name="project",
    )(dq, terms, cosine, sine, w_query, key_weight, value_weight, far_weight)


def local(
    n_ctx,
    n_tp,
    query,
    key_projected,
    value,
    attention_output,
    output_gradient,
    lse,
    block_mask,
    positions,
    segments,
    w_query,
    key_weight,
    value_weight,
):
    tok_rows = query.shape[0]
    q_start = lax.axis_index("ctx") * tok_rows
    cosine, sine = rope_tables(positions, HEAD_SIZE)
    kv_blocks, *prepared, far_weight = gather(
        n_ctx, n_tp, key_projected, value, query, output_gradient, attention_output, cosine, sine,
        key_weight, value_weight,
    )
    kv_whole = kv_blocks.reshape(n_ctx * tok_rows, kv_blocks.shape[-1])
    seg_row = lax.dynamic_slice_in_dim(segments, q_start, tok_rows).reshape(1, tok_rows)
    first_tile = (q_start // TILE).astype(jnp.int32).reshape(1)
    query_grad, terms = attention(
        first_tile, block_mask, prepared, lse, cosine, sine, kv_whole, seg_row
    )
    return project(
        n_ctx, n_tp, query_grad, terms, cosine, sine, w_query, key_weight, value_weight, far_weight
    )


def solution(mesh):
    in_specs = (
        P("ctx", "tp"),
        P("ctx", "tp"),
        P("ctx", "tp"),
        P("ctx", "tp"),
        P("ctx", "tp"),
        P("tp", "ctx"),
        P(),
        P("ctx"),
        P(),
        P(None, "tp"),
        P(None, "tp"),
        P(None, "tp"),
    )
    out_specs = P("tp", "ctx")
    body = functools.partial(local, mesh.shape["ctx"], mesh.shape["tp"])
    return jax.shard_map(body, mesh=mesh, in_specs=in_specs, out_specs=out_specs, check_vma=False)
```
